128 devices in a mesh: dp: 32 (over x, y, core), mp: 4 (over z).
Axes of the slice: x: 4, y: 4, z: 4, core: 2. Of those that a mesh axis runs over, the one named last changes fastest.
Arguments:
- attention_output: bfloat16 [16384, 4096], P('dp', 'mp'), may hold values from -6 to 6
- residual: bfloat16 [16384, 4096], P('dp', 'mp')
- output_projection_weight: bfloat16 [4096, 4096], P(None, 'mp'), may hold values from -0.09375 to 0.09375
- adapter_down_matrix: bfloat16 [4096, 16], replicated, may hold values from -0.09375 to 0.09375
- adapter_up_matrix: bfloat16 [16, 4096], P(None, 'mp'), may hold values from -1.5 to 1.5
- final_norm_gain: bfloat16 [4096], P('mp'), may hold values from 0.5 to 1.5
- query_hidden_states: bfloat16 [1024, 4096], P('dp', 'mp')
- pair_passage_index: int32 [1024, 17], P('dp'), may hold values from 0 to 4095, as said below
- lengths: int32 [4096], P('dp'), may hold values from 1 to 4
Outputs:
- per_query_loss: float32 [1024], P('dp')
- query_gradient: bfloat16 [1024, 4096], P('dp', 'mp')
- residual_gradient: bfloat16 [16384, 4096], P('dp', 'mp')
- attention_gradient: bfloat16 [16384, 4096], P('dp', 'mp')
- down_matrix_gradient: float32 [4096, 16], P('mp')
- up_matrix_gradient: float32 [16, 4096], P(None, 'mp')
The draws below stay inside these ranges and needn't reach their ends.
Inputs may be any that keep to these rules, and one draw needn't show every extreme that they name: `pair_passage_index`: passage p is held at dp index p // 128. Among the 544 entries of one device's rows (aligned blocks of 32 rows), at most 25 name passages of any one owner; in every block exactly 25 name passages of one owner, the same owner for all blocks.
All inputs are finite; a program needn't handle non-finite values.
Results may differ from the reference program's by a relative error of at most 0.03.
Values may be sent and summed in bfloat16 or wider, within the bound.
No kernel may reach another device: no remote copies, remote signals or barrier semaphores. Data moves between devices by JAX's collectives and lax.ppermute only.
A program may use at most 128 MiB of HBM per device.

```python
import math
import jax
import jax.numpy as jnp
from jax import lax

MODEL_WIDTH = 4096
ADAPTER_RANK = 16
HARD = 17
Q_DEV = 32
PASS_DEV = 128
SEQ = 4
QUERIES = 1024
PASSAGES = 4096
TOKENS = 16384
CAP = 25
N_DP = 32


def scale_rows(key, base):
    factor = jnp.exp(jax.random.uniform(key, (base.shape[0], 1), minval=math.log(0.5), maxval=math.log(8.0)))
    return (base * factor).astype(jnp.bfloat16)


def draw_residual(key, part):
    key = jax.random.fold_in(key, 3)
    first, second = jax.random.split(key, 2)
    base = jnp.clip(jax.random.normal(second, (TOKENS, MODEL_WIDTH)), -4.0, 4.0)
    return scale_rows(first, base)


def draw_query_hidden_states(key, part):
    key = jax.random.fold_in(key, 5)
    first, second = jax.random.split(key, 2)
    base = jnp.clip(jax.random.normal(second, (QUERIES, MODEL_WIDTH)), -4.0, 4.0)
    return scale_rows(first, base)


def draw_pair_passage_index(key, part):
    key = jax.random.fold_in(key, 7)
    hot_key, block_root = jax.random.split(key)
    hot_owner = jax.random.randint(hot_key, (), 0, N_DP)
    per_block = Q_DEV * HARD

    def one_block(block_key):
        first, second, third = jax.random.split(block_key, 3)
        offset = jax.random.randint(first, (), 0, N_DP - 1)
        place = jnp.arange(per_block)
        others = (hot_owner + 1 + (place - CAP + offset) % (N_DP - 1)) % N_DP
        owner_ids = jnp.where(place < CAP, hot_owner, others)
        owner_ids = owner_ids[jax.random.permutation(second, per_block)]
        local_rows = jax.random.randint(third, (per_block,), 0, PASS_DEV)
        return owner_ids * PASS_DEV + local_rows
    block_keys = jax.random.split(block_root, N_DP)
    return jax.vmap(one_block)(block_keys).reshape(N_DP * Q_DEV, HARD).astype(jnp.int32)


def place_ends(array, key, low, largest):
    longest = array.shape.index(max(array.shape))
    spots = []
    for shift in (0, 1):
        where = [jax.random.randint(jax.random.fold_in(key, axis), (), 0, length) for axis, length in enumerate(array.shape)]
        where[longest] = (where[longest] + shift) % array.shape[longest]
        spots.append(tuple(where))
    return array.at[spots[0]].set(low).at[spots[1]].set(largest)


def shard_levels(own_key, extent, cuts, least, top_value):
    def one(dim, blocks):
        steps = jax.random.uniform(jax.random.fold_in(jax.random.fold_in(own_key, 6), dim), (blocks,), jnp.float32, least / len(cuts), top_value / len(cuts))
        return jnp.repeat(jnp.exp(steps), extent[dim] // blocks).reshape((-1,) + (1,) * (len(extent) - dim - 1))

    loudness = one(*cuts[0])
    for cut in cuts[1:]:
        loudness = loudness * one(*cut)
    return loudness


def gaussian(key, shape, deviation, limit, pieces=(), dtype=jnp.bfloat16):
    array = jax.random.normal(key, shape, jnp.float32) * deviation
    if len(pieces) > 0:
        array = shard_levels(key, shape, pieces, -0.22, 0.18) * array
    return jnp.clip(array, min=-limit, max=limit).astype(dtype)


def setup_inputs(seed: int = 0) -> dict:
    key_list = jax.random.split(jax.random.key(seed), 10)
    attention_output = gaussian(key_list[0], (TOKENS, MODEL_WIDTH), 1.0, 6.0, ((0, 32), (1, 4)))
    residual = draw_residual(jax.random.fold_in(key_list[9], 71), 0)
    output_projection_weight = gaussian(key_list[2], (MODEL_WIDTH, MODEL_WIDTH), MODEL_WIDTH ** -0.5, 0.09375, ((1, 4),))
    adapter_down_matrix = gaussian(key_list[3], (MODEL_WIDTH, ADAPTER_RANK), MODEL_WIDTH ** -0.5, 0.09375)
    adapter_up_matrix = gaussian(key_list[4], (ADAPTER_RANK, MODEL_WIDTH), ADAPTER_RANK ** -0.5, 1.5, ((1, 4),))
    final_norm_gain = jnp.clip(1.0 + 0.1 * jax.random.normal(key_list[5], (MODEL_WIDTH,), jnp.float32), 0.5, 1.5).astype(jnp.bfloat16)
    query_hidden_states = draw_query_hidden_states(jax.random.fold_in(key_list[9], 71), 0)
    pair_passage_index = draw_pair_passage_index(jax.random.fold_in(key_list[9], 71), 0)
    lengths = place_ends(jax.random.randint(key_list[8], (PASSAGES,), 1, SEQ + 1), jax.random.fold_in(key_list[8], 1), 1, SEQ).astype(jnp.int32)
    return {"attention_output": attention_output, "residual": residual, "output_projection_weight": output_projection_weight, "adapter_down_matrix": adapter_down_matrix, "adapter_up_matrix": adapter_up_matrix, "final_norm_gain": final_norm_gain, "query_hidden_states": query_hidden_states, "pair_passage_index": pair_passage_index, "lengths": lengths}


SOFTMAX_TEMPER = 0.02
LOSS_SCALE = 1024.0

def reference(attention_output, residual, output_projection_weight, adapter_down_matrix, adapter_up_matrix, final_norm_gain, query_hidden_states, pair_passage_index, lengths):
    single_float = jnp.float32
    adapter_middle = jnp.dot(attention_output, adapter_down_matrix, preferred_element_type=single_float).astype(jnp.bfloat16)
    residual_stream = residual.astype(single_float) + jnp.dot(attention_output, output_projection_weight, preferred_element_type=single_float) + 2.0 * jnp.dot(adapter_middle, adapter_up_matrix, preferred_element_type=single_float)
    inverse_rms = lax.rsqrt(lax.optimization_barrier(jnp.sum(residual_stream * residual_stream, axis=1, keepdims=True)) / MODEL_WIDTH + 1e-05)
    gain_f32 = final_norm_gain.astype(single_float)
    normed = residual_stream * inverse_rms * gain_f32
    valid = (jnp.arange(SEQ)[None, :] < lengths[:, None]).astype(single_float)
    length_f32 = lengths.astype(single_float)[:, None]
    pooled = lax.optimization_barrier(jnp.sum(normed.reshape(PASSAGES, SEQ, MODEL_WIDTH) * valid[:, :, None], axis=1)) / length_f32
    pooled_f32 = pooled.astype(jnp.bfloat16).astype(single_float)
    query_f32 = query_hidden_states.astype(single_float)
    passage_inverse = lax.rsqrt(lax.optimization_barrier(jnp.sum(pooled_f32 * pooled_f32, axis=1)) + 1e-06)
    query_inverse = lax.rsqrt(lax.optimization_barrier(jnp.sum(query_f32 * query_f32, axis=1)) + 1e-06)
    hard_rows = pooled_f32[pair_passage_index]
    negative_inverse = passage_inverse[pair_passage_index]
    negative_product = jnp.einsum('qkd,qd->qk', hard_rows, query_f32, precision=lax.Precision.HIGHEST)
    negative_logits = negative_product * query_inverse[:, None] * negative_inverse / SOFTMAX_TEMPER
    query_blocks = query_f32.reshape(N_DP, Q_DEV, MODEL_WIDTH)
    pass_blocks = pooled_f32.reshape(N_DP, PASS_DEV, MODEL_WIDTH)
    batch_product = jnp.einsum('nqd,npd->nqp', query_blocks, pass_blocks, precision=lax.Precision.HIGHEST).reshape(QUERIES, PASS_DEV)
    batch_inverse = jnp.repeat(passage_inverse.reshape(N_DP, 1, PASS_DEV), Q_DEV, axis=1).reshape(QUERIES, PASS_DEV)
    batch_logits = batch_product * query_inverse[:, None] * batch_inverse / SOFTMAX_TEMPER
    log_total = jnp.log(lax.optimization_barrier(jnp.sum(jnp.exp(negative_logits), axis=1)) + lax.optimization_barrier(jnp.sum(jnp.exp(batch_logits), axis=1)))
    per_query_loss = log_total - negative_logits[:, 0]
    positive = (jnp.arange(HARD) == 0).astype(single_float)
    negative_coefficient = LOSS_SCALE * (jnp.exp(negative_logits - log_total[:, None]) - positive[None, :])
    batch_coefficient = LOSS_SCALE * jnp.exp(batch_logits - log_total[:, None])
    negative_softmax_weight = (negative_coefficient * query_inverse[:, None] * negative_inverse / SOFTMAX_TEMPER).astype(jnp.bfloat16).astype(single_float)
    batch_softmax_weight = (batch_coefficient * query_inverse[:, None] * batch_inverse / SOFTMAX_TEMPER).astype(jnp.bfloat16).astype(single_float)
    query_scalar = lax.optimization_barrier(jnp.sum(negative_coefficient * negative_logits, axis=1)) + lax.optimization_barrier(jnp.sum(batch_coefficient * batch_logits, axis=1))
    weight_blocks = batch_softmax_weight.reshape(N_DP, Q_DEV, PASS_DEV)
    toward_query = jnp.einsum('qk,qkd->qd', negative_softmax_weight, hard_rows, precision=lax.Precision.HIGHEST)
    toward_query = toward_query + jnp.einsum('nqp,npd->nqd', weight_blocks, pass_blocks, precision=lax.Precision.HIGHEST).reshape(QUERIES, MODEL_WIDTH)
    query_gradient = (toward_query - (query_scalar * query_inverse * query_inverse)[:, None] * query_f32).astype(jnp.bfloat16)
    flat_ids = pair_passage_index.reshape(-1).astype(jnp.int32)
    hard_terms = (negative_softmax_weight[:, :, None] * query_f32[:, None, :]).reshape(QUERIES * HARD, MODEL_WIDTH)
    home_terms = jax.ops.segment_sum(hard_terms, flat_ids, num_segments=PASSAGES)
    home_scalars = jax.ops.segment_sum((negative_coefficient * negative_logits).reshape(-1), flat_ids, num_segments=PASSAGES)
    batch_to_pass = jnp.einsum('nqp,nqd->npd', weight_blocks, query_blocks, precision=lax.Precision.HIGHEST).reshape(PASSAGES, MODEL_WIDTH)
    pass_scalar = home_scalars + lax.optimization_barrier(jnp.sum((batch_coefficient * batch_logits).reshape(N_DP, Q_DEV, PASS_DEV), axis=1)).reshape(PASSAGES)
    grad_pooled = home_terms + batch_to_pass - (pass_scalar * passage_inverse * passage_inverse)[:, None] * pooled_f32
    grad_normed = ((grad_pooled / length_f32)[:, None, :] * valid[:, :, None]).reshape(TOKENS, MODEL_WIDTH)
    gain_grad = gain_f32 * grad_normed
    inner_sum = lax.optimization_barrier(jnp.sum(residual_stream * gain_grad, axis=1, keepdims=True))
    grad_stream = inverse_rms * gain_grad - residual_stream * inverse_rms ** 3 * inner_sum / MODEL_WIDTH
    residual_gradient = grad_stream.astype(jnp.bfloat16)
    adapter_backward = (2.0 * jnp.dot(residual_gradient, adapter_up_matrix.T, preferred_element_type=single_float)).astype(jnp.bfloat16)
    attention_gradient = (jnp.dot(residual_gradient, output_projection_weight.T, preferred_element_type=single_float) + jnp.dot(adapter_backward, adapter_down_matrix.T, preferred_element_type=single_float)).astype(jnp.bfloat16)
    down_matrix_gradient = jnp.dot(attention_output.T, adapter_backward, preferred_element_type=single_float)
    up_matrix_gradient = 2.0 * jnp.dot(adapter_middle.T, residual_gradient, preferred_element_type=single_float)
    return (per_query_loss, query_gradient, residual_gradient, attention_gradient, down_matrix_gradient, up_matrix_gradient)
```

```python
import jax
import jax.numpy as jnp
from jax import lax
from jax.experimental import pallas as pl
from jax.experimental.pallas import tpu as pltpu
from jax.sharding import PartitionSpec as P

F32 = jnp.float32
BF16 = jnp.bfloat16
INV_TEMPER = 1.0 / 0.02
LOSS_SCALE = 1024.0
SLOTS = 32
PAIRS = [(a, b) for a in range(4) for b in range(a, 4)]


def dot(a, b, dims):
    return lax.dot_general(a, b, ((dims[0], dims[1]), ((), ())), preferred_element_type=F32)


def split3(x):
    a = x.astype(BF16).astype(F32)
    b = (x - a).astype(BF16).astype(F32)
    return [a, b, x - a - b]


def iota(shape, dim):
    return lax.broadcasted_iota(jnp.int32, shape, dim)


def stack_rows(rows, height):
    where = iota((height, rows[0].shape[1]), 0)
    total = jnp.zeros((height, rows[0].shape[1]), F32)
    for place, row in enumerate(rows):
        total = jnp.where(where == place, row, total)
    return total


def decode(code):
    used = code > 0
    value = code - 1
    return used, value >> 8, (value >> 1) & 127, value & 1


def partial_kernel(stream, qslot, qown, code, squares, gain, pack):
    used, _, passage, _ = decode(code[...])
    onehot = (iota((128, 1024), 0) == passage) & used
    g = gain[...]
    columns = []
    scaled = []
    for s in range(4):
        x = stream[s * 128 : s * 128 + 128, :]
        u = x * g
        scaled.append(u)
        columns.append(jnp.sum(x * x, axis=1, keepdims=True))
        ub = u.astype(BF16)
        scores = dot(ub, qslot[...], ((1,), (1,)))
        pack[16 + s : 17 + s, :] = jnp.sum(jnp.where(onehot, scores, 0.0), axis=0, keepdims=True)
        batch = dot(qown[...], ub, ((1,), (1,)))
        pack[0:16, s * 128 : s * 128 + 128] = batch[0:16]
        pack[0:16, 512 + s * 128 : 640 + s * 128] = batch[16:32]
    for a, b in PAIRS:
        columns.append(jnp.sum(scaled[a] * scaled[b], axis=1, keepdims=True))
    lane = iota((128, 128), 1)
    table = jnp.zeros((128, 128), F32)
    for place, column in enumerate(columns):
        table = jnp.where(lane == place, column, table)
    table = table.T
    pack[20:21, :] = squares[0:1, :]
    pack[21:23, :] = jnp.zeros((2, 1024), F32)
    for place in range(len(columns)):
        row, off = 21 + place // 8, (place % 8) * 128
        pack[row : row + 1, off : off + 128] = table[place : place + 1, :]
    pack[23:24, :] = squares[1:2, :]


def score_kernel(p0, p1, p2, p3, code, lens, home, slot, batch, stats, sums):
    def total(rows, lanes):
        return (p0[rows, lanes] + p2[rows, lanes]) + (p1[rows, lanes] + p3[rows, lanes])

    def stat(place):
        row, off = 21 + place // 8, (place % 8) * 128
        return total(slice(row, row + 1), slice(off, off + 128))

    every = slice(0, 1024)
    used, query, passage, first = decode(code[...])
    length = lens[...]
    inv = [lax.rsqrt(stat(s) / 4096.0 + 1e-05) for s in range(4)]
    a = [jnp.where(s < length, inv[s] / length, 0.0) for s in range(4)]
    gram = {pair: stat(4 + i) for i, pair in enumerate(PAIRS)}
    toward = [
        sum(a[t] * gram[(min(s, t), max(s, t))] for t in range(4)) for s in range(4)
    ]
    square = sum(a[s] * toward[s] for s in range(4))
    pinv = lax.rsqrt(square + 1e-06)
    rows = []
    for row in a + [pinv]:
        rows += split3(row)
    onehot = jnp.where((iota((128, 1024), 0) == passage) & used, 1.0, 0.0).astype(BF16)
    picked = dot(stack_rows(rows, 16).astype(BF16), onehot, ((1,), (0,)))
    pick = [
        picked[3 * i : 3 * i + 1] + picked[3 * i + 1 : 3 * i + 2] + picked[3 * i + 2 : 3 * i + 3]
        for i in range(5)
    ]
    dots = [total(slice(16 + s, 17 + s), every) for s in range(4)]
    product = pick[0] * dots[0] + pick[1] * dots[1] + pick[2] * dots[2] + pick[3] * dots[3]
    qinv = lax.rsqrt(total(slice(20, 21), every) + 1e-06)
    pre = qinv * pick[4] * INV_TEMPER
    score = product * pre
    grown = jnp.where(used, jnp.exp(score), 0.0)
    slot[0:1, :] = score
    slot[1:2, :] = pre
    for s in range(4):
        slot[2 + s : 3 + s, :] = dots[s]
    slot[6:8, :] = jnp.zeros((2, 1024), F32)

    own = total(slice(23, 24), slice(0, 128))
    lane = iota((32, 128), 1)
    qcol = lax.rsqrt(
        jnp.sum(jnp.where(lane == iota((32, 128), 0), own, 0.0), axis=1, keepdims=True) + 1e-06
    )
    pieces = []
    for s in range(4):
        top = total(slice(0, 16), slice(s * 128, s * 128 + 128))
        low = total(slice(0, 16), slice(512 + s * 128, 640 + s * 128))
        pieces.append(jnp.concatenate([top, low], axis=0))
        batch[:, 256 + s * 128 : 384 + s * 128] = pieces[s]
    bpre = qcol * pinv * INV_TEMPER
    bscore = sum(a[s] * pieces[s] for s in range(4)) * bpre
    bgrown = jnp.exp(bscore)
    batch[:, 0:128] = bscore
    batch[:, 128:256] = bpre

    stats[...] = stack_rows(a + inv + toward + [pinv], 16)

    mine = iota((32, 1024), 0) == query
    block = ((iota((1024, 128), 0) >> 5) == iota((1024, 128), 1)).astype(F32).astype(BF16)

    def by_query(row):
        out = jnp.zeros((32, 128), F32)
        for part in split3(row):
            out += dot(jnp.where(mine, part, 0.0).astype(BF16), block, ((1,), (0,)))
        return out

    at_home = lane == home[...]
    exp_sum = by_query(grown) + jnp.where(at_home, jnp.sum(bgrown, axis=1, keepdims=True), 0.0)
    weighted = by_query(grown * score) + jnp.where(
        at_home, jnp.sum(bgrown * bscore, axis=1, keepdims=True), 0.0
    )
    positive = by_query(jnp.where(used & (first == 1), score, 0.0))
    sums[:, 0:128] = exp_sum
    sums[:, 128:256] = weighted
    sums[:, 256:384] = positive
    sums[:, 384:512] = jnp.broadcast_to(qcol, (32, 128))


def gradient_kernel(
    recv, stream, qslot, qown, gain, code, slot, batch, stats, home,
    grad, weights, pooled_out, bweights, logs, scratch,
):
    used, query, passage, first = decode(code[...])
    log_row = jnp.log(jnp.sum(recv[:, 0:1024], axis=0, keepdims=True))
    spread = iota((32, 1024), 0) == (iota((32, 1024), 1) >> 5)
    place = ((iota((1024, 128), 0) & 31) == iota((1024, 128), 1)).astype(F32).astype(BF16)
    table = jnp.zeros((32, 128), F32)
    for part in split3(log_row):
        table += dot(jnp.where(spread, part, 0.0).astype(BF16), place, ((1,), (0,)))
    block = (iota((128, 1024), 0) == (iota((128, 1024), 1) >> 5)).astype(F32).astype(BF16)
    wide = jnp.zeros((32, 1024), F32)
    for part in split3(table):
        wide += dot(part.astype(BF16), block, ((1,), (0,)))
    log_slot = jnp.sum(jnp.where(iota((32, 1024), 0) == query, wide, 0.0), axis=0, keepdims=True)
    log_col = jnp.sum(jnp.where(iota((32, 128), 1) == home[...], table, 0.0), axis=1, keepdims=True)
    logs[...] = jnp.broadcast_to(log_col, (32, 128))

    score = slot[0:1, :]
    coef = jnp.where(used, LOSS_SCALE * (jnp.exp(score - log_slot) - first.astype(F32)), 0.0)
    weight = (coef * slot[1:2, :]).astype(BF16).astype(F32)
    bscore = batch[:, 0:128]
    bcoef = LOSS_SCALE * jnp.exp(bscore - log_col)
    bweight = (bcoef * batch[:, 128:256]).astype(BF16).astype(F32)
    bweights[...] = bweight.astype(BF16)
    onehot = (iota((128, 1024), 0) == passage) & used
    spread_weight = jnp.where(onehot, weight, 0.0)
    wb = spread_weight.astype(BF16)
    weights[...] = wb
    scalar = jnp.sum(jnp.where(onehot, coef * score, 0.0), axis=1, keepdims=True)

    rows = [jnp.sum(bcoef * bscore, axis=0, keepdims=True)]
    for s in range(4):
        rows.append(
            jnp.sum(bweight * batch[:, 256 + s * 128 : 384 + s * 128], axis=0, keepdims=True)
        )
    rows += [stats[i : i + 1, :] for i in range(13)]
    cols = stack_rows(rows, 128).T

    def col(i):
        return cols[:, i : i + 1]

    pinv = col(17)
    scale = (scalar + col(0)) * pinv * pinv
    g = gain[...]
    xs = [stream[s * 128 : s * 128 + 128, :] for s in range(4)]
    pooled = sum(col(5 + s) * (xs[s] * g) for s in range(4)).astype(BF16)
    pooled_out[...] = pooled
    gp = dot(wb, qslot[...], ((1,), (0,)))
    bt = jnp.concatenate([bweight, jnp.zeros((96, 128), F32)], axis=0).T.astype(BF16)
    qpad = jnp.concatenate([qown[...], jnp.zeros((96, 1024), BF16)], axis=0)
    gp = gp + dot(bt, qpad, ((1,), (0,))) - scale * pooled.astype(F32)
    gg = gp * g
    for s in range(4):
        a, inv = col(5 + s), col(9 + s)
        inner = (
            jnp.sum(spread_weight * slot[2 + s : 3 + s, :], axis=1, keepdims=True)
            + col(1 + s)
            - scale * col(13 + s)
        )
        beta = inv * inv * a * inner / 4096.0
        scratch[s * 128 : s * 128 + 128, :] = (a * gg - beta * xs[s]).astype(BF16)
    token = iota((512, 512), 0)
    order = ((token & 3) * 128 + (token >> 2) == iota((512, 512), 1)).astype(F32).astype(BF16)
    grad[...] = dot(order, scratch[...], ((1,), (0,))).astype(BF16)


def call(kernel, outs, *args, scratch=()):
    return pl.pallas_call(
        kernel,
        out_shape=[jax.ShapeDtypeStruct(s, t) for s, t in outs],
        in_specs=[pl.BlockSpec(memory_space=pltpu.VMEM)] * len(args),
        out_specs=[pl.BlockSpec(memory_space=pltpu.VMEM)] * len(outs),
        scratch_shapes=list(scratch),
        compiler_params=pltpu.CompilerParams(vmem_limit_bytes=40 * 2**20),
    )(*args)


def ring(x, step):
    return lax.ppermute(x, "mp", [(i, (i + step) % 4) for i in range(4)])


def ring_sum(x):
    return (x + ring(x, 2)) + (ring(x, 1) + ring(x, 3))


def grid_index(x, y, core):
    return (x * 4 + y) * 2 + core


def grid_shift(v, axis, step):
    pairs = []
    for x in range(4):
        for y in range(4):
            for core in range(2):
                if axis == "core":
                    to = (x, y, 1 - core)
                elif axis == "x":
                    to = ((x + step) % 4, y, core)
                else:
                    to = (x, (y + step) % 4, core)
                pairs.append((grid_index(x, y, core), grid_index(*to)))
    return lax.ppermute(v, "dp", pairs)


def grid_sum(x):
    x = x.astype(BF16)
    x = (x.astype(F32) + grid_shift(x, "core", 1).astype(F32)).astype(BF16)
    for axis in ("x", "y"):
        parts = [x] + [grid_shift(x, axis, step) for step in (1, 2, 3)]
        parts = [p.astype(F32) for p in parts]
        x = (parts[0] + parts[2]) + (parts[1] + parts[3])
        x = x.astype(BF16) if axis == "x" else x
    return x


def body(
    attention_output,
    residual,
    output_projection_weight,
    adapter_down_matrix,
    adapter_up_matrix,
    final_norm_gain,
    query_hidden_states,
    pair_passage_index,
    lengths,
):
    me = lax.axis_index("mp")
    home = jnp.full((1, 128), lax.axis_index("dp"), jnp.int32)
    half = 256

    def rows_of(matrix, offset):
        return lax.dynamic_slice_in_dim(matrix, ((me + offset) % 4) * 1024, 1024, 0)

    top, low = attention_output[:half], attention_output[half:]
    left_top, right_low = ring(top, 1), ring(low, 3)
    left_low, right_top = ring(low, 1), ring(top, 3)
    far_top, far_low = ring(left_top, 1), ring(right_low, 3)

    flat = pair_passage_index.reshape(-1)
    entries = flat.shape[0]
    place = jnp.arange(entries)
    owned = (flat[None, :] >> 7) == jnp.arange(32)[:, None]
    before = (place[:, None] < place[None, :]).astype(BF16)
    rank = dot(owned.astype(BF16), before, ((1,), (0,))).astype(jnp.int32)
    value = 1 + 2 * (128 * (place // 17) + (flat & 127)) + (place % 17 == 0)
    rank = jnp.where(owned, rank, -1)
    code_out = jnp.sum(
        jnp.where(rank[:, None, :] == jnp.arange(SLOTS)[None, :, None], value[None, None, :], 0),
        axis=2,
    )
    used_out, query_out, _, _ = decode(code_out)
    hot = (used_out[:, :, None] & (query_out[:, :, None] == jnp.arange(32))).reshape(1024, 32)
    hot_b = hot.astype(BF16)
    qslot_out = dot(hot_b, query_hidden_states, ((1,), (0,))).astype(BF16)
    query_f32 = query_hidden_states.astype(F32)
    own_square = jnp.sum(query_f32 * query_f32, axis=1)
    slot_square = jnp.sum(jnp.where(hot, own_square[None, :], 0.0), axis=1).reshape(32, SLOTS)
    table = lax.all_to_all(
        jnp.concatenate([code_out.astype(F32), slot_square], axis=1), "dp", 0, 0, tiled=True
    )
    code = table[:, :SLOTS].reshape(1, 1024).astype(jnp.int32)
    squares = jnp.concatenate(
        [table[:, SLOTS:].reshape(1, 1024), jnp.pad(own_square, (0, 992)).reshape(1, 1024)], axis=0
    )
    qslot = lax.all_to_all(qslot_out, "dp", 0, 0, tiled=True)

    middle = ring_sum(dot(rows_of(adapter_down_matrix, 0), attention_output, ((0,), (1,))))
    middle = middle.astype(BF16)
    weight = output_projection_weight
    row = iota((512, 512), 0)
    order = ((row & 127) * 4 + (row >> 7) == iota((512, 512), 1)).astype(BF16)

    def ordered(x):
        return dot(order, x, ((1,), (0,))).astype(BF16)

    stream = ordered(residual).astype(F32)
    stream = stream + dot(ordered(attention_output), rows_of(weight, 0), ((1,), (0,)))
    middle_ordered = dot(order, middle, ((1,), (1,))).astype(BF16)
    stream = stream + 2.0 * dot(middle_ordered, adapter_up_matrix, ((1,), (0,)))
    left = ordered(jnp.concatenate([left_top, left_low], 0))
    stream = stream + dot(left, rows_of(weight, 3), ((1,), (0,)))
    right = ordered(jnp.concatenate([right_top, right_low], 0))
    stream = stream + dot(right, rows_of(weight, 1), ((1,), (0,)))
    far_block = ordered(jnp.concatenate([far_top, far_low], 0))
    stream = stream + dot(far_block, rows_of(weight, 2), ((1,), (0,)))

    gain = final_norm_gain.astype(F32).reshape(1, 1024)
    (pack,) = call(
        partial_kernel,
        [((24, 1024), F32)],
        stream, qslot, query_hidden_states, code, squares, gain,
    )
    packs = [pack, ring(pack, 1), ring(pack, 2), ring(pack, 3)]
    lens = lengths.astype(F32).reshape(1, 128)
    slot, batch, stats, sums = call(
        score_kernel,
        [((8, 1024), F32), ((32, 768), F32), ((16, 128), F32), ((32, 512), F32)],
        *packs, code, lens, home,
    )
    exp_sums = jnp.broadcast_to(sums[:, 0:32].reshape(1, 1024), (32, 1024))
    recv = lax.all_to_all(
        jnp.concatenate([exp_sums, sums[:, 128:160].T, sums[:, 256:288].T], axis=1),
        "dp", 0, 0, tiled=True,
    )
    grad, weights, pooled, bweights, logs = call(
        gradient_kernel,
        [((512, 1024), BF16), ((128, 1024), BF16), ((128, 1024), BF16), ((32, 128), BF16), ((32, 128), F32)],
        recv, stream, qslot, query_hidden_states, gain, code, slot, batch, stats, home,
        scratch=[pltpu.VMEM((512, 1024), BF16)],
    )

    def back(offset, lo, hi):
        return dot(grad[lo:hi], rows_of(weight, offset), ((1,), (1,)))

    far = back(2, 0, 512).astype(BF16)
    via_right, via_left = ring(far[:half], 1), ring(far[half:], 3)
    to_right_low = ring(back(1, half, 512).astype(BF16), 1)
    to_left_top = ring(back(3, 0, half).astype(BF16), 3)
    to_right_top = ring((back(1, 0, half) + via_right.astype(F32)).astype(BF16), 1)
    to_left_low = ring((back(3, half, 512) + via_left.astype(F32)).astype(BF16), 3)

    rows = dot(weights, pooled, ((0,), (0,))).astype(BF16)
    arrived = lax.all_to_all(rows, "dp", 0, 0, tiled=True)
    others = jnp.sum(recv[:, 1024:1088], axis=0)
    log_total, positive = logs[:, 0], others[32:64]
    per_query_loss = log_total - positive
    query_scalar = LOSS_SCALE * (others[0:32] * jnp.exp(-log_total) - positive)
    qinv = sums[:, 384]
    query_gradient = (
        dot(hot_b, arrived, ((0,), (0,)))
        + dot(bweights, pooled, ((1,), (0,)))
        - (query_scalar * qinv * qinv)[:, None] * query_f32
    ).astype(BF16)

    lora_back = (2.0 * ring_sum(dot(adapter_up_matrix, grad, ((1,), (1,))))).astype(BF16)
    down_part = dot(lora_back, attention_output, ((1,), (0,)))
    up_part = dot(middle, grad, ((1,), (0,)))
    adapter = grid_sum(jnp.concatenate([down_part, up_part], axis=0))
    local = dot(lora_back, rows_of(adapter_down_matrix, 0), ((0,), (1,)))
    own = back(0, 0, 512) + local
    from_left = jnp.concatenate([to_right_top, to_right_low], 0).astype(F32)
    from_right = jnp.concatenate([to_left_top, to_left_low], 0).astype(F32)
    attention_gradient = (own + from_left + from_right).astype(BF16)
    return (
        per_query_loss,
        query_gradient,
        grad,
        attention_gradient,
        adapter[0:16].T,
        2.0 * adapter[16:32],
    )


def solution(mesh):
    in_specs = (
        P("dp", "mp"),
        P("dp", "mp"),
        P(None, "mp"),
        P(),
        P(None, "mp"),
        P("mp"),
        P("dp", "mp"),
        P("dp", None),
        P("dp"),
    )
    out_specs = (P("dp"), P("dp", "mp"), P("dp", "mp"), P("dp", "mp"), P("mp", None), P(None, "mp"))
    return jax.shard_map(body, mesh=mesh, in_specs=in_specs, out_specs=out_specs, check_vma=False)
```

```python
import jax
import jax.numpy as jnp
from jax import lax
from jax.experimental import pallas as pl
from jax.experimental.pallas import tpu as pltpu
from jax.sharding import PartitionSpec as P

F32 = jnp.float32
BF16 = jnp.bfloat16
INV_TEMPER = 1.0 / 0.02
LOSS_SCALE = 1024.0
SLOTS = 32
HARD = 17
PAIRS = [(a, b) for a in range(4) for b in range(a, 4)]


def dot(a, b, dims):
    return lax.dot_general(a, b, ((dims[0], dims[1]), ((), ())), preferred_element_type=F32)


def split3(x):
    a = x.astype(BF16).astype(F32)
    b = (x - a).astype(BF16).astype(F32)
    return [a, b, x - a - b]


def iota(shape, dim):
    return lax.broadcasted_iota(jnp.int32, shape, dim)


def stack_rows(rows, height):
    where = iota((height, rows[0].shape[1]), 0)
    total = jnp.zeros((height, rows[0].shape[1]), F32)
    for place, row in enumerate(rows):
        total = jnp.where(where == place, row, total)
    return total


def step_of(offset):
    return lax.rem(lax.axis_index("mp") + offset, 4)


class Fetch:
    def __init__(self, weight, buffer, sems, offset):
        base = step_of(offset) * 1024
        self.buffer = buffer
        self.copies = [
            pltpu.make_async_copy(
                weight.at[pl.ds(pl.multiple_of(base + k * 256, 256), 256), :],
                buffer.at[pl.ds(k * 256, 256), :],
                sems.at[k],
            )
            for k in range(4)
        ]
        for copy in self.copies:
            copy.start()

    def wait(self, k):
        self.copies[k].wait()


def move(source, target, sems, part):
    rows = pl.ds(part * 128, 128)
    copy = pltpu.make_async_copy(source.at[rows, :], target.at[rows, :], sems.at[part])
    copy.start()
    return copy


def down_rows(down, offset):
    return down[:, pl.ds(pl.multiple_of(step_of(offset) * 1024, 1024), 1024)]


def forward_dot(blocks, fetch, first):
    out = list(first)
    for k in range(4):
        fetch.wait(k)
        part = fetch.buffer[k * 256 : k * 256 + 256, :]
        for i, block in enumerate(blocks):
            out[i] = out[i] + dot(block[:, k * 256 : k * 256 + 256], part, ((1,), (0,)))
    return out


def order_kernel(tokens, top, low):
    for i, out in enumerate((top, low)):
        row = iota((256, 512), 0) + i * 256
        order = ((row & 127) * 4 + (row >> 7) == iota((256, 512), 1)).astype(F32).astype(BF16)
        out[...] = dot(order, tokens[...], ((1,), (0,))).astype(BF16)


def slot_kernel(ids_row, ids_col, queries, out, home):
    ids = ids_row[...]
    owner = iota((32, 640), 0)
    owned = (ids >> 7) == owner
    before = (iota((640, 640), 0) < iota((640, 640), 1)).astype(F32).astype(BF16)
    rank = dot(owned.astype(F32).astype(BF16), before, ((1,), (0,)))
    slot = jnp.sum(jnp.where(owned, rank + (owner * SLOTS).astype(F32), 0.0), axis=0, keepdims=True)
    slot = jnp.where(ids < 0, -1.0, slot).astype(jnp.int32)
    listed = (iota((1024, 640), 0) == slot).astype(F32).astype(BF16)
    entry, lane = iota((640, 128), 0), iota((640, 128), 1)
    query = (entry * 241) >> 12
    values = jnp.where(lane < 32, (query == lane).astype(F32), 0.0)
    values = jnp.where(lane == 32, (ids_col[...] & 127).astype(F32), values)
    values = jnp.where((lane == 33) & (query * HARD == entry), 1.0, values)
    values = jnp.where(lane == 34, 1.0, values)
    picked = dot(listed, values.astype(BF16), ((1,), (0,)))
    q = queries[...].astype(F32)
    squares = jnp.sum(q * q, axis=1, keepdims=True)
    square_row = jnp.sum(
        jnp.where(iota((32, 128), 0) == iota((32, 128), 1), squares, 0.0), axis=0, keepdims=True
    )
    lane = iota((1024, 128), 1)
    mine = jnp.where(lane < 32, picked, 0.0)
    square = jnp.sum(mine * square_row, axis=1, keepdims=True)
    for i, part in enumerate(split3(square)):
        picked = jnp.where(lane == 35 + i, part, picked)
    home[...] = picked.T[0:40, :]
    padded = jnp.concatenate([queries[...], jnp.zeros((96, 1024), BF16)], axis=0)
    out[:, 0:1024] = dot(mine.astype(BF16), padded, ((1,), (0,))).astype(BF16)
    out[:, 1024:1152] = picked.astype(BF16)


def meta_kernel(qslot, meta, turned):
    turned[...] = qslot[:, 0:1024].astype(F32).T.astype(BF16)
    table = qslot[:, 1024:1152].astype(F32).T
    meta[0:40, :] = table[0:40, :]
    meta[35:36, :] = table[35:36, :] + table[36:37, :] + table[37:38, :]


def own_kernel(top, low, residual, weight, down, stream, middle, buffer, sems):
    fetch = Fetch(weight, buffer, sems, 0)
    first = []
    for i in range(2):
        row = iota((256, 512), 0) + i * 256
        order = ((row & 127) * 4 + (row >> 7) == iota((256, 512), 1)).astype(F32).astype(BF16)
        first.append(dot(order, residual[...], ((1,), (0,))))
    d = down_rows(down, 0)
    middle[:, 0:256] = dot(d, top[...], ((1,), (1,)))
    middle[:, 256:512] = dot(d, low[...], ((1,), (1,)))
    out = forward_dot([top, low], fetch, first)
    stream[0:256, :] = out[0]
    stream[256:512, :] = out[1]


def sides_kernel(
    left_top, left_low, right_top, right_low, before, middle_before, weight, down,
    stream, middle, buffer, buffer2, sems, sems2,
):
    fetch = Fetch(weight, buffer, sems, 3)
    fetch2 = Fetch(weight, buffer2, sems2, 1)
    d, d2 = down_rows(down, 3), down_rows(down, 1)
    middle[:, 0:256] = (
        middle_before[:, 0:256]
        + dot(d, left_top[...], ((1,), (1,)))
        + dot(d2, right_top[...], ((1,), (1,)))
    )
    middle[:, 256:512] = (
        middle_before[:, 256:512]
        + dot(d, left_low[...], ((1,), (1,)))
        + dot(d2, right_low[...], ((1,), (1,)))
    )
    out = forward_dot([left_top, left_low], fetch, [before[0:256, :], before[256:512, :]])
    out = forward_dot([right_top, right_low], fetch2, out)
    stream[0:256, :] = out[0]
    stream[256:512, :] = out[1]


def listed_onehot(meta):
    return (iota((128, 1024), 0).astype(F32) == meta[32:33, :]) & (meta[34:35, :] > 0.0)


def partial_kernel(
    far_top, far_low, before, middle_before, weight, down, up, turned, qown, meta, gain,
    pack, stream_out, middle, buffer, sems, tokens, stream, out_sems,
):
    fetch = Fetch(weight, buffer, sems, 2)
    d = down_rows(down, 2)
    mid = [
        (middle_before[:, i * 256 : i * 256 + 256] + dot(d, far[...], ((1,), (1,)))).astype(BF16)
        for i, far in enumerate((far_top, far_low))
    ]
    out = [
        before[i * 256 : i * 256 + 256, :] + 2.0 * dot(mid[i], up[...], ((0,), (0,)))
        for i in range(2)
    ]
    middle[:, 0:256] = mid[0]
    middle[:, 256:512] = mid[1]
    out = forward_dot([far_top, far_low], fetch, out)
    onehot = listed_onehot(meta)
    g = gain[...]
    columns = []
    scaled = []
    sent = []
    for s in range(4):
        x = out[s // 2][(s % 2) * 128 : (s % 2) * 128 + 128]
        stream[s * 128 : s * 128 + 128, :] = x
        sent.append(move(stream, stream_out, out_sems, s))
        u = x * g
        scaled.append(u)
        columns.append(jnp.sum(x * x, axis=1, keepdims=True))
        tokens[s * 128 : s * 128 + 128, :] = u.astype(BF16)
    batch = dot(qown[...], tokens[...], ((1,), (1,)))
    pack[0:16, 0:512] = batch[0:16]
    pack[0:16, 512:1024] = batch[16:32]
    for j in range(4):
        lanes = slice(j * 256, j * 256 + 256)
        scores = dot(tokens[...], turned[:, lanes], ((1,), (0,)))
        for s in range(4):
            pack[16 + s : 17 + s, lanes] = jnp.sum(
                jnp.where(onehot[:, lanes], scores[s * 128 : s * 128 + 128], 0.0),
                axis=0,
                keepdims=True,
            )
    for a, b in PAIRS:
        columns.append(jnp.sum(scaled[a] * scaled[b], axis=1, keepdims=True))
    lane = iota((128, 128), 1)
    table = jnp.zeros((128, 128), F32)
    for place, column in enumerate(columns):
        table = jnp.where(lane == place, column, table)
    table = table.T
    pack[20:21, :] = meta[35:36, :]
    pack[21:23, :] = jnp.zeros((2, 1024), F32)
    for place in range(len(columns)):
        row, off = 21 + place // 8, (place % 8) * 128
        pack[row : row + 1, off : off + 128] = table[place : place + 1, :]
    q = qown[...].astype(F32)
    squares = jnp.sum(q * q, axis=1, keepdims=True)
    pack[23:24, 0:128] = jnp.sum(
        jnp.where(iota((32, 128), 0) == iota((32, 128), 1), squares, 0.0), axis=0, keepdims=True
    )
    pack[23:24, 128:1024] = jnp.zeros((1, 896), F32)
    for copy in sent:
        copy.wait()


def score_kernel(p0, p1, p2, p3, meta, lens, slot, batch, stats, sums):
    def total(rows, lanes):
        return (p0[rows, lanes] + p2[rows, lanes]) + (p1[rows, lanes] + p3[rows, lanes])

    def stat(place):
        row, off = 21 + place // 8, (place % 8) * 128
        return total(slice(row, row + 1), slice(off, off + 128))

    every = slice(0, 1024)
    used = meta[34:35, :] > 0.0
    length = lens[...].astype(F32)
    inv = [lax.rsqrt(stat(s) / 4096.0 + 1e-05) for s in range(4)]
    a = [jnp.where(s < length, inv[s] / length, 0.0) for s in range(4)]
    gram = {pair: stat(4 + i) for i, pair in enumerate(PAIRS)}
    toward = [
        sum(a[t] * gram[(min(s, t), max(s, t))] for t in range(4)) for s in range(4)
    ]
    square = sum(a[s] * toward[s] for s in range(4))
    pinv = lax.rsqrt(square + 1e-06)
    rows = []
    for row in a + [pinv]:
        rows += split3(row)
    onehot = jnp.where(listed_onehot(meta), 1.0, 0.0).astype(BF16)
    picked = dot(stack_rows(rows, 16).astype(BF16), onehot, ((1,), (0,)))
    pick = [
        picked[3 * i : 3 * i + 1] + picked[3 * i + 1 : 3 * i + 2] + picked[3 * i + 2 : 3 * i + 3]
        for i in range(5)
    ]
    dots = [total(slice(16 + s, 17 + s), every) for s in range(4)]
    product = pick[0] * dots[0] + pick[1] * dots[1] + pick[2] * dots[2] + pick[3] * dots[3]
    qinv = lax.rsqrt(total(slice(20, 21), every) + 1e-06)
    pre = qinv * pick[4] * INV_TEMPER
    score = product * pre
    grown = jnp.where(used, jnp.exp(score), 0.0)
    slot[0:1, :] = score
    slot[1:2, :] = pre
    for s in range(4):
        slot[2 + s : 3 + s, :] = dots[s]
    slot[6:8, :] = jnp.zeros((2, 1024), F32)

    own = total(slice(23, 24), slice(0, 128))
    lane = iota((32, 128), 1)
    qcol = lax.rsqrt(
        jnp.sum(jnp.where(lane == iota((32, 128), 0), own, 0.0), axis=1, keepdims=True) + 1e-06
    )
    pieces = []
    for s in range(4):
        top = total(slice(0, 16), slice(s * 128, s * 128 + 128))
        low = total(slice(0, 16), slice(512 + s * 128, 640 + s * 128))
        pieces.append(jnp.concatenate([top, low], axis=0))
        batch[:, 256 + s * 128 : 384 + s * 128] = pieces[s]
    bpre = qcol * pinv * INV_TEMPER
    bscore = sum(a[s] * pieces[s] for s in range(4)) * bpre
    bgrown = jnp.exp(bscore)
    batch[:, 0:128] = bscore
    batch[:, 128:256] = bpre
    batch[:, 768:896] = jnp.broadcast_to(qcol, (32, 128))

    stats[...] = stack_rows(a + inv + toward + [pinv], 16)

    mine = meta[0:32, :]
    block = ((iota((1024, 128), 0) >> 5) == iota((1024, 128), 1)).astype(F32).astype(BF16)

    def by_query(row):
        out = jnp.zeros((32, 128), F32)
        for part in split3(row):
            out += dot((mine * part).astype(BF16), block, ((1,), (0,)))
        return out

    at_home = lane == lax.axis_index("dp")
    exp_sum = by_query(grown) + jnp.where(at_home, jnp.sum(bgrown, axis=1, keepdims=True), 0.0)
    place = ((iota((128, 1024), 1) & 31) == iota((128, 1024), 0)).astype(F32).astype(BF16)
    wide = jnp.zeros((32, 1024), F32)
    for part in split3(exp_sum):
        wide += dot(part.astype(BF16), place, ((1,), (0,)))
    spread = iota((32, 1024), 0) == (iota((32, 1024), 1) >> 5)
    exp_row = jnp.sum(jnp.where(spread, wide, 0.0), axis=0, keepdims=True)
    for b in range(32):
        group = slice(b // 4 * 128, b // 4 * 128 + 128)
        sums[b, :, 0:1024] = exp_row
        sums[b, :, 1024:1152] = score[:, group]
        sums[b, :, 1152:1280] = pre[:, group]


def pooled_kernel(stream_in, stats, gain, qslot, pooled, rows, stream, sems):
    for copy in [move(stream_in, stream, sems, s) for s in range(4)]:
        copy.wait()
    cols = jnp.concatenate([stats[...], jnp.zeros((112, 128), F32)], axis=0).T
    g = gain[...]
    mean = sum(cols[:, s : s + 1] * (stream[s * 128 : s * 128 + 128, :] * g) for s in range(4))
    pooled[...] = mean.astype(BF16)
    meta = qslot[:, 1024:1152].astype(F32)
    lane = iota((1024, 128), 1).astype(F32)
    listed = ((meta[:, 32:33] == lane) & (meta[:, 34:35] > 0.0)).astype(F32).astype(BF16)
    rows[...] = dot(listed, pooled[...], ((1,), (0,))).astype(BF16)


def gradient_kernel(
    recv, stream_in, qslot, qown, gain, meta, slot, batch, stats, pooled, up, middle, weight,
    grad_out, far_top, far_low, lora, extras_out, up_part,
    buffer, sems, stream, in_sems, grad, out_sems, extras, extras_sem, ordered,
):
    arriving = [move(stream_in, stream, in_sems, s) for s in range(4)]
    fetch = Fetch(weight, buffer, sems, 2)
    total = recv[0, :, 0:1024]
    for b in range(1, 32):
        total = total + recv[b, :, 0:1024]
    log_row = jnp.log(total)
    spread = iota((32, 1024), 0) == (iota((32, 1024), 1) >> 5)
    place = ((iota((1024, 128), 0) & 31) == iota((1024, 128), 1)).astype(F32).astype(BF16)
    table = jnp.zeros((32, 128), F32)
    for part in split3(log_row):
        table += dot(jnp.where(spread, part, 0.0).astype(BF16), place, ((1,), (0,)))
    block = (iota((128, 1024), 0) == (iota((128, 1024), 1) >> 5)).astype(F32).astype(BF16)
    wide = jnp.zeros((32, 1024), F32)
    for part in split3(table):
        wide += dot(part.astype(BF16), block, ((1,), (0,)))
    log_slot = jnp.sum(meta[0:32, :] * wide, axis=0, keepdims=True)
    lane = iota((32, 128), 1)
    log_col = jnp.sum(
        jnp.where(lane == lax.axis_index("dp"), table, 0.0), axis=1, keepdims=True
    )
    extras[:, 0:128] = jnp.broadcast_to(log_col, (32, 128))
    used, first = meta[34:35, :] > 0.0, meta[33:34, :]
    score = slot[0:1, :]
    coef = jnp.where(used, LOSS_SCALE * (jnp.exp(score - log_slot) - first), 0.0)
    value = (coef * slot[1:2, :]).astype(BF16).astype(F32)
    bscore = batch[:, 0:128]
    bcoef = LOSS_SCALE * jnp.exp(bscore - log_col)
    bweight = (bcoef * batch[:, 128:256]).astype(BF16).astype(F32)
    extras[:, 128:256] = bweight
    extras[:, 256:384] = bcoef * bscore
    extras_copy = pltpu.make_async_copy(extras, extras_out, extras_sem.at[0])
    extras_copy.start()
    onehot = listed_onehot(meta)
    spread_weight = jnp.where(onehot, value, 0.0)
    wb = spread_weight.astype(BF16)
    scalar = jnp.sum(jnp.where(onehot, coef * score, 0.0), axis=1, keepdims=True)

    rows = [jnp.sum(bcoef * bscore, axis=0, keepdims=True)]
    for s in range(4):
        rows.append(
            jnp.sum(bweight * batch[:, 256 + s * 128 : 384 + s * 128], axis=0, keepdims=True)
        )
    rows += [stats[i : i + 1, :] for i in range(13)]
    cols = stack_rows(rows, 128).T

    def col(i):
        return cols[:, i : i + 1]

    pinv = col(17)
    scale = (scalar + col(0)) * pinv * pinv
    g = gain[...]
    gp = dot(wb, qslot[:, 0:1024], ((1,), (0,)))
    bt = jnp.concatenate([bweight, jnp.zeros((96, 128), F32)], axis=0).T.astype(BF16)
    qpad = jnp.concatenate([qown[...], jnp.zeros((96, 1024), BF16)], axis=0)
    gp = gp + dot(bt, qpad, ((1,), (0,))) - scale * pooled[...].astype(F32)
    gg = gp * g
    leaving = [extras_copy]
    for s in range(4):
        arriving[s].wait()
        x = stream[s * 128 : s * 128 + 128, :]
        a, inv = col(5 + s), col(9 + s)
        inner = (
            jnp.sum(spread_weight * slot[2 + s : 3 + s, :], axis=1, keepdims=True)
            + col(1 + s)
            - scale * col(13 + s)
        )
        beta = inv * inv * a * inner / 4096.0
        ordered[s * 128 : s * 128 + 128, :] = (a * gg - beta * x).astype(BF16)
    token = iota((512, 512), 0)
    order = ((token & 3) * 128 + (token >> 2) == iota((512, 512), 1)).astype(F32).astype(BF16)
    grad[...] = dot(order, ordered[...], ((1,), (0,))).astype(BF16)
    leaving += [move(grad, grad_out, out_sems, s) for s in range(4)]
    lora[...] = dot(up[...], grad[...], ((1,), (1,)))
    up_part[...] = dot(middle[...], ordered[...], ((1,), (0,)))
    for k in range(4):
        fetch.wait(k)
        for i, out in enumerate((far_top, far_low)):
            out[:, k * 256 : k * 256 + 256] = dot(
                grad[i * 256 : i * 256 + 256, :], buffer[k * 256 : k * 256 + 256, :], ((1,), (1,))
            ).astype(BF16)
    for copy in leaving:
        copy.wait()


def sides_back_kernel(
    grad_in, weight,
    right_low, left_top, right_top, left_low,
    buffer, buffer2, sems, sems2, grad, in_sems,
):
    arriving = [move(grad_in, grad, in_sems, s) for s in range(4)]
    fetch = Fetch(weight, buffer, sems, 1)
    fetch2 = Fetch(weight, buffer2, sems2, 3)
    for copy in arriving:
        copy.wait()
    for fetched, low, top in ((fetch, right_low, right_top), (fetch2, left_low, left_top)):
        for k in range(4):
            fetched.wait(k)
            part = fetched.buffer[k * 256 : k * 256 + 256, :]
            columns = slice(k * 256, k * 256 + 256)
            top[:, columns] = dot(grad[0:256, :], part, ((1,), (1,))).astype(top.dtype)
            low[:, columns] = dot(grad[256:512, :], part, ((1,), (1,))).astype(low.dtype)


def join_kernel(l0, l1, l2, l3, tokens, up_part, adapter, lora_back):
    lora = (2.0 * ((l0[...] + l2[...]) + (l1[...] + l3[...]))).astype(BF16)
    lora_back[...] = lora
    adapter[0:16, :] = dot(lora, tokens[...], ((1,), (0,))).astype(BF16)
    adapter[16:32, :] = up_part[...].astype(BF16)


def add_kernel(right_top, left_low, via_right, via_left, to_right, to_left):
    to_right[...] = (right_top[...].astype(F32) + via_right[...].astype(F32)).astype(BF16)
    to_left[...] = (left_low[...].astype(F32) + via_left[...].astype(F32)).astype(BF16)


def pair_kernel(a, b, out):
    out[...] = (a[...].astype(F32) + b[...].astype(F32)).astype(BF16)


def four_sum(parts):
    a, b, c, d = [part[...].astype(F32) for part in parts]
    return (a + c) + (b + d)


def four_kernel(a, b, c, d, out):
    out[...] = four_sum((a, b, c, d)).astype(BF16)


def last_kernel(a, b, c, d, down, up):
    total = four_sum((a, b, c, d))
    down[...] = total[0:16]
    up[...] = 2.0 * total[16:32]


def finish_kernel(before, from_left, from_right, out):
    out[0:256, :] = (before[0:256, :] + from_left[...].astype(F32)).astype(BF16)
    out[256:512, :] = (before[256:512, :] + from_right[...].astype(F32)).astype(BF16)


def own_back_kernel(
    grad_in, weight, down, lora_back, from_right, from_left, out, buffer, sems, grad, in_sems
):
    arriving = [move(grad_in, grad, in_sems, s) for s in range(4)]
    fetch = Fetch(weight, buffer, sems, 0)
    local = dot(lora_back[...], down_rows(down, 0), ((0,), (0,)))
    for copy in arriving:
        copy.wait()
    for k in range(4):
        fetch.wait(k)
        lanes = slice(k * 256, k * 256 + 256)
        own = local[:, lanes] + dot(grad[...], buffer[k * 256 : k * 256 + 256, :], ((1,), (1,)))
        out[0:256, lanes] = own[0:256] + from_right[:, lanes].astype(F32)
        out[256:512, lanes] = own[256:512] + from_left[:, lanes].astype(F32)


def query_kernel(
    recv, home, extras, batch, pooled, qown, arrived, gradient, loss
):
    group = lax.rem(lax.axis_index("dp"), 4) * 32
    place = iota((128, 1024), 0) == (iota((128, 1024), 1) & 31) + group
    place = place.astype(F32).astype(BF16)
    spread = iota((32, 1024), 0) == (iota((32, 1024), 1) >> 5)
    sub = iota((32, 128), 0)

    def by_slot(lanes):
        table = jnp.zeros((32, 128), F32)
        for d in range(32):
            table = jnp.where(sub == d, recv[d, :, lanes], table)
        wide = jnp.zeros((32, 1024), F32)
        for part in split3(table):
            wide += dot(part.astype(BF16), place, ((1,), (0,)))
        return jnp.sum(jnp.where(spread, wide, 0.0), axis=0, keepdims=True)

    score, pre = by_slot(slice(1024, 1152)), by_slot(slice(1152, 1280))
    mine, first, used = home[0:32, :], home[33:34, :], home[34:35, :] > 0.0
    log_col = extras[:, 0:1]
    log_slot = jnp.sum(mine * log_col, axis=0, keepdims=True)
    coef = jnp.where(used, LOSS_SCALE * (jnp.exp(score - log_slot) - first), 0.0)
    value = jnp.where(used, coef * pre, 0.0).astype(BF16).astype(F32)
    score = jnp.where(used, score, 0.0)
    positive = jnp.sum(mine * (first * score), axis=1, keepdims=True)
    scalar = jnp.sum(mine * (coef * score), axis=1, keepdims=True)
    scalar = scalar + jnp.sum(extras[:, 256:384], axis=1, keepdims=True)
    eye = iota((32, 128), 0) == iota((32, 128), 1)
    row = jnp.sum(jnp.where(eye, log_col - positive, 0.0), axis=0, keepdims=True)
    loss[...] = row[:, 0:32]
    qinv = batch[:, 768:769]
    total = dot((mine * value).astype(BF16), arrived[...], ((1,), (0,)))
    total = total + dot(extras[:, 128:256].astype(BF16), pooled[...], ((1,), (0,)))
    gradient[...] = (total - (scalar * qinv * qinv) * qown[...].astype(F32)).astype(BF16)


ANY, HOLD, LOAD, STORE = "any", "hold", "load", "store"


def call(kernel, outs, args, scratch=(), limit=16, cost=None):
    in_specs, values, moved = [], [], []
    for place, arg in enumerate(args):
        space = pltpu.VMEM
        if isinstance(arg, tuple):
            arg, mark = arg
            space = pltpu.HBM
            if mark != ANY:
                arg = pltpu.with_memory_space_constraint(arg, pltpu.HBM)
            if mark == LOAD:
                moved.append((place, arg.shape, arg.dtype))
        values.append(arg)
        in_specs.append(pl.BlockSpec(memory_space=space))
    loads = len(moved)
    for place, (shape, dtype, *mark) in enumerate(outs):
        if mark == [STORE]:
            moved.append((len(args) + place, shape, dtype))
    count, extra = len(args) + len(outs), len(moved)

    def whole(*refs):
        refs = list(refs)
        if not extra:
            return kernel(*refs)
        sems = refs.pop()
        buffers = [refs.pop() for _ in range(extra)][::-1]
        copies = []
        for i, (place, _, _) in enumerate(moved):
            ends = (refs[place], buffers[i]) if i < loads else (buffers[i], refs[place])
            copies.append(pltpu.make_async_copy(*ends, sems.at[i]))
            refs[place] = buffers[i]
        for copy in copies[:loads]:
            copy.start()
        for copy in copies[:loads]:
            copy.wait()
        kernel(*refs)
        for copy in copies[loads:]:
            copy.start()
        for copy in copies[loads:]:
            copy.wait()

    scratch = list(scratch)
    if extra:
        scratch += [pltpu.VMEM(shape, dtype) for _, shape, dtype in moved]
        scratch.append(pltpu.SemaphoreType.DMA((extra,)))
    if cost is not None:
        cost = pl.CostEstimate(flops=int(cost * 1.15e9), bytes_accessed=0, transcendentals=0)
    return pl.pallas_call(
        whole,
        cost_estimate=cost,
        name=kernel.__name__,
        out_shape=[
            (pltpu.HBM if mark else jax.ShapeDtypeStruct)(s, t) for s, t, *mark in outs
        ],
        in_specs=in_specs,
        out_specs=[
            pl.BlockSpec(memory_space=pltpu.HBM if mark else pltpu.VMEM) for _, _, *mark in outs
        ],
        scratch_shapes=scratch,
        compiler_params=pltpu.CompilerParams(vmem_limit_bytes=limit * 2**20),
    )(*values)


COST_OWN = 20.0
COST_PAIR = 3.0
COST_JOIN = 16.0
COST_GRAD = 1.0
COST_SIDES = 1.0
WEIGHT_BUFFER = pltpu.VMEM((1024, 1024), BF16)
FOUR = pltpu.SemaphoreType.DMA((4,))


def ring(x, step):
    return lax.ppermute(x, "mp", [(i, (i + step) % 4) for i in range(4)])


def ring_sum(x):
    return (x + ring(x, 2)) + (ring(x, 1) + ring(x, 3))


def grid_index(x, y, core):
    return (x * 4 + y) * 2 + core


def grid_shift(v, axis, step):
    pairs = []
    for x in range(4):
        for y in range(4):
            for core in range(2):
                if axis == "core":
                    to = (x, y, 1 - core)
                elif axis == "x":
                    to = ((x + step) % 4, y, core)
                else:
                    to = (x, (y + step) % 4, core)
                pairs.append((grid_index(x, y, core), grid_index(*to)))
    return lax.ppermute(v, "dp", pairs)


def grid_sum(x, own, query):
    shape = x.shape
    tie = lax.optimization_barrier
    (x,) = call(pair_kernel, [(shape, BF16)], [x, grid_shift(x, "core", 1)], cost=COST_PAIR)
    parts = [x] + [grid_shift(x, "x", step) for step in (1, 2, 3)]
    own, *parts = tie((own, *parts))
    (x,) = call(four_kernel, [(shape, BF16)], parts)
    parts = [x] + [grid_shift(x, "y", step) for step in (1, 2, 3)]
    query, own, *parts = tie((query, own, *parts))
    down, up = call(last_kernel, [((16, 1024), F32), ((16, 1024), F32)], parts)
    return down, up, own, query


def body(
    attention_output,
    residual,
    output_projection_weight,
    adapter_down_matrix,
    adapter_up_matrix,
    final_norm_gain,
    query_hidden_states,
    pair_passage_index,
    lengths,
):
    weight = (output_projection_weight, HOLD)
    down = adapter_down_matrix.T
    up = adapter_up_matrix
    qown = query_hidden_states
    half, full = (256, 1024), (512, 1024)
    tie = lax.optimization_barrier

    top, low = call(
        order_kernel, [(half, BF16), (half, BF16)], [(attention_output, LOAD)]
    )
    with jax.named_scope("leg1"):
        left_top, right_low = ring(top, 1), ring(low, 3)

    ids, _, _ = tie((pair_passage_index, top, low))
    flat = jnp.pad(ids.reshape(-1), (0, 640 - 544), constant_values=-1)
    qslot_out, home = call(
        slot_kernel,
        [((1024, 1152), BF16, STORE), ((40, 1024), F32, STORE)],
        [flat.reshape(1, 640), flat.reshape(640, 1), qown],
    )
    with jax.named_scope("a2a_queries"):
        qslot = lax.all_to_all(qslot_out, "dp", 0, 0, tiled=True)
    with jax.named_scope("leg2"):
        left_low, right_top = ring(low, 1), ring(top, 3)
    with jax.named_scope("leg3"):
        far_top, far_low = ring(left_top, 1), ring(right_low, 3)

    residual_tied, left_top, right_low = tie((residual, left_top, right_low))
    stream, middle = call(
        own_kernel,
        [(full, F32), ((16, 512), F32)],
        [top, low, residual_tied, weight, down],
        [WEIGHT_BUFFER, FOUR], limit=24, cost=COST_OWN,
    )
    stream, middle = call(
        sides_kernel,
        [(full, F32), ((16, 512), F32)],
        [left_top, left_low, right_top, right_low, stream, middle, weight, down],
        [WEIGHT_BUFFER, WEIGHT_BUFFER, FOUR, FOUR], limit=24,
    )
    gain = final_norm_gain.astype(F32).reshape(1, 1024)
    meta, turned = call(
        meta_kernel,
        [((40, 1024), F32), ((1024, 1024), BF16)],
        [qslot],
    )
    pack, stream, middle = call(
        partial_kernel,
        [((24, 1024), F32), (full, F32, ANY), ((16, 512), BF16)],
        [far_top, far_low, stream, middle, weight, down, up, turned, qown, meta, gain],
        [WEIGHT_BUFFER, FOUR, pltpu.VMEM((512, 1024), BF16), pltpu.VMEM(full, F32), FOUR], limit=24,
    )
    with jax.named_scope("packs"):
        packs = [pack, ring(pack, 1), ring(pack, 2), ring(pack, 3)]
    slot, batch, stats, sums = call(
        score_kernel,
        [((8, 1024), F32), ((32, 896), F32), ((16, 128), F32), ((32, 1, 1280), F32)],
        [*packs, meta, lengths.reshape(1, 128)],
    )
    with jax.named_scope("a2a_sums"):
        recv = lax.all_to_all(sums, "dp", 0, 0, tiled=True)
    pooled, rows = call(
        pooled_kernel,
        [((128, 1024), BF16), ((1024, 1024), BF16)],
        [(stream, ANY), stats, gain, qslot],
        [pltpu.VMEM(full, F32), FOUR],
    )
    grad, far_top, far_low, lora, extras, up_part = call(
        gradient_kernel,
        [
            (full, BF16, ANY), (half, BF16), (half, BF16), ((16, 512), F32),
            ((32, 384), F32, ANY), ((16, 1024), F32),
        ],
        [recv, (stream, ANY), qslot, qown, gain, meta, slot, batch, stats, pooled, up, middle, weight],
        [
            WEIGHT_BUFFER, FOUR, pltpu.VMEM(full, F32), FOUR, pltpu.VMEM(full, BF16), FOUR,
            pltpu.VMEM((32, 384), F32), pltpu.SemaphoreType.DMA((1,)), pltpu.VMEM(full, BF16),
        ],
        limit=24, cost=COST_GRAD,
    )

    far_top, far_low, rows = tie((far_top, far_low, rows))
    with jax.named_scope("back1"):
        via_right, via_left = ring(far_top, 1), ring(far_low, 3)
    with jax.named_scope("lora_sum"):
        loras = [lora, ring(lora, 1), ring(lora, 2), ring(lora, 3)]
    with jax.named_scope("a2a_rows"):
        arrived = lax.all_to_all(rows, "dp", 0, 0, tiled=True)
    right_low, left_top, right_top, left_low = call(
        sides_back_kernel,
        [(half, BF16), (half, BF16), (half, BF16), (half, BF16)],
        [(grad, ANY), weight],
        [WEIGHT_BUFFER, WEIGHT_BUFFER, FOUR, FOUR, pltpu.VMEM(full, BF16), FOUR],
        limit=24,
        cost=COST_SIDES,
    )
    with jax.named_scope("back2"):
        to_right_low, to_left_top = ring(right_low, 1), ring(left_top, 3)
    right_top, left_low = call(
        add_kernel,
        [(half, BF16), (half, BF16)],
        [right_top, left_low, via_right, via_left],
    )
    right_top, left_low, up_part = tie((right_top, left_low, up_part))
    adapter, lora_back = call(
        join_kernel,
        [((32, 1024), BF16), ((16, 512), BF16)],
        [*loras, (attention_output, LOAD), up_part],
        cost=COST_JOIN,
    )
    with jax.named_scope("back3"):
        to_right_top, to_left_low = ring(right_top, 1), ring(left_low, 3)
    (before,) = call(
        own_back_kernel,
        [(full, F32)],
        [(grad, ANY), weight, down, lora_back, to_left_top, to_right_low],
        [WEIGHT_BUFFER, FOUR, pltpu.VMEM(full, BF16), FOUR],
        limit=24,
    )
    query_gradient, loss = call(
        query_kernel,
        [((32, 1024), BF16), ((1, 32), F32)],
        [
            (recv, LOAD), (home, LOAD), (extras, LOAD), (batch, LOAD), (pooled, LOAD),
            (qown, LOAD), arrived,
        ],
    )
    with jax.named_scope("adapters"):
        down_grad, up_grad, before, query_gradient = grid_sum(adapter, before, query_gradient)
    (attention_gradient,) = call(
        finish_kernel,
        [(full, BF16)],
        [before, to_right_top, to_left_low],
    )
    return (
        loss.reshape(32),
        query_gradient,
        grad,
        attention_gradient,
        down_grad.T,
        up_grad,
    )


def solution(mesh):
    in_specs = (
        P("dp", "mp"),
        P("dp", "mp"),
        P(None, "mp"),
        P(),
        P(None, "mp"),
        P("mp"),
        P("dp", "mp"),
        P("dp", None),
        P("dp"),
    )
    out_specs = (P("dp"), P("dp", "mp"), P("dp", "mp"), P("dp", "mp"), P("mp", None), P(None, "mp"))
    return jax.shard_map(body, mesh=mesh, in_specs=in_specs, out_specs=out_specs, check_vma=False)
```

```python
import jax
import jax.numpy as jnp
from jax import lax
from jax.experimental import pallas as pl
from jax.experimental.pallas import tpu as pltpu
from jax.sharding import PartitionSpec as P

F32 = jnp.float32
BF16 = jnp.bfloat16
INV_TEMPER = 1.0 / 0.02
LOSS_SCALE = 1024.0
SLOTS = 32
HARD = 17
PAIRS = [(a, b) for a in range(4) for b in range(a, 4)]


def dot(a, b, dims):
    return lax.dot_general(a, b, ((dims[0], dims[1]), ((), ())), preferred_element_type=F32)


def split3(x):
    a = x.astype(BF16).astype(F32)
    b = (x - a).astype(BF16).astype(F32)
    return [a, b, x - a - b]


def iota(shape, dim):
    return lax.broadcasted_iota(jnp.int32, shape, dim)


def stack_rows(rows, height):
    where = iota((height, rows[0].shape[1]), 0)
    total = jnp.zeros((height, rows[0].shape[1]), F32)
    for place, row in enumerate(rows):
        total = jnp.where(where == place, row, total)
    return total


def step_of(offset):
    return lax.rem(lax.axis_index("mp") + offset, 4)


class Fetch:
    def __init__(self, weight, buffer, sems, offset):
        base = step_of(offset) * 1024
        self.buffer = buffer
        self.copies = [
            pltpu.make_async_copy(
                weight.at[pl.ds(pl.multiple_of(base + k * 256, 256), 256), :],
                buffer.at[pl.ds(k * 256, 256), :],
                sems.at[k],
            )
            for k in range(4)
        ]
        for copy in self.copies:
            copy.start()

    def wait(self, k):
        self.copies[k].wait()


def move(source, target, sems, part):
    rows = pl.ds(part * 128, 128)
    copy = pltpu.make_async_copy(source.at[rows, :], target.at[rows, :], sems.at[part])
    copy.start()
    return copy


def down_rows(down, offset):
    return down[:, pl.ds(pl.multiple_of(step_of(offset) * 1024, 1024), 1024)]


def forward_dot(blocks, fetch, first):
    out = list(first)
    for k in range(4):
        fetch.wait(k)
        part = fetch.buffer[k * 256 : k * 256 + 256, :]
        for i, block in enumerate(blocks):
            out[i] = out[i] + dot(block[:, k * 256 : k * 256 + 256], part, ((1,), (0,)))
    return out


def order_kernel(tokens, top, low):
    for i, out in enumerate((top, low)):
        row = iota((256, 512), 0) + i * 256
        order = ((row & 127) * 4 + (row >> 7) == iota((256, 512), 1)).astype(F32).astype(BF16)
        out[...] = dot(order, tokens[...], ((1,), (0,))).astype(BF16)


def fold_map(shape, slot_dim):
    part = iota(shape, 1 - slot_dim)
    return iota(shape, slot_dim) == (part & 31) * 24 + (part >> 5)


def fold(pieces, last, out):
    width = last.shape[1]
    off = 0
    for piece in pieces:
        lanes = slice(off, off + piece.shape[1])
        for o in range(32):
            out[o * 24 : o * 24 + 24, lanes] = piece[o * 32 : o * 32 + 24].astype(BF16)
        off += piece.shape[1]
    stack = jnp.concatenate([last[:, i : i + 128] for i in range(0, width, 128)], axis=0)
    table = fold_map((768, stack.shape[0]), 0).astype(F32).astype(BF16)
    out[:, width : width + 128] = dot(table, stack, ((1,), (0,))).astype(BF16)


def unfold(arrived, full):
    width = full.shape[1]
    parts = width // 128
    table = fold_map((parts * 32, 768), 1).astype(F32).astype(BF16)
    stack = dot(table, arrived[:, width : width + 128], ((1,), (0,))).astype(BF16)
    last = jnp.concatenate([stack[c * 32 : c * 32 + 32] for c in range(parts)], axis=1)
    last = jnp.concatenate([last, jnp.zeros((96, width), BF16)], axis=0)
    place = (iota((256, 128), 0) == iota((256, 128), 1) * 8).astype(F32).astype(BF16)
    rows = dot(place, last, ((1,), (0,))).astype(BF16)
    for b in range(32):
        full[b * 32 : b * 32 + 24, :] = arrived[b * 24 : b * 24 + 24, 0:width]
        full[b * 32 + 24 : b * 32 + 32, :] = rows[b * 8 : b * 8 + 8]


def last_slots():
    return (iota((32, 1024), 1) == iota((32, 1024), 0) * 32 + 24).astype(F32).astype(BF16)


def slot_kernel(ids_row, ids_col, queries, out, home):
    ids = ids_row[...]
    owner = iota((32, 640), 0)
    owned = (ids >> 7) == owner
    before = (iota((640, 640), 0) < iota((640, 640), 1)).astype(F32).astype(BF16)
    rank = dot(owned.astype(F32).astype(BF16), before, ((1,), (0,)))
    slot = jnp.sum(jnp.where(owned, rank + (owner * SLOTS).astype(F32), 0.0), axis=0, keepdims=True)
    slot = jnp.where(ids < 0, -1.0, slot).astype(jnp.int32)
    listed = (iota((1024, 640), 0) == slot).astype(F32).astype(BF16)
    entry, lane = iota((640, 128), 0), iota((640, 128), 1)
    query = (entry * 241) >> 12
    values = jnp.where(lane < 32, (query == lane).astype(F32), 0.0)
    values = jnp.where(lane == 32, (ids_col[...] & 127).astype(F32), values)
    values = jnp.where((lane == 33) & (query * HARD == entry), 1.0, values)
    values = jnp.where(lane == 34, 1.0, values)
    picked = dot(listed, values.astype(BF16), ((1,), (0,)))
    q = queries[...].astype(F32)
    squares = jnp.sum(q * q, axis=1, keepdims=True)
    square_row = jnp.sum(
        jnp.where(iota((32, 128), 0) == iota((32, 128), 1), squares, 0.0), axis=0, keepdims=True
    )
    lane = iota((1024, 128), 1)
    mine = jnp.where(lane < 32, picked, 0.0)
    square = jnp.sum(mine * square_row, axis=1, keepdims=True)
    for i, part in enumerate(split3(square)):
        picked = jnp.where(lane == 35 + i, part, picked)
    home[...] = picked.T[0:40, :]
    padded = jnp.concatenate([queries[...], jnp.zeros((96, 1024), BF16)], axis=0)
    rows = dot(mine.astype(BF16), padded, ((1,), (0,)))
    last = dot(last_slots(), mine.astype(BF16), ((1,), (0,))).astype(BF16)
    last = dot(last, padded, ((1,), (0,))).astype(BF16)
    last_values = dot(last_slots(), picked.astype(BF16), ((1,), (0,))).astype(BF16)
    fold([rows, picked], jnp.concatenate([last, last_values], axis=1), out)


def meta_kernel(arrived, qslot, meta, turned):
    unfold(arrived, qslot)
    turned[...] = qslot[:, 0:1024].astype(F32).T.astype(BF16)
    table = qslot[:, 1024:1152].astype(F32).T
    meta[0:40, :] = table[0:40, :]
    meta[35:36, :] = table[35:36, :] + table[36:37, :] + table[37:38, :]


def own_kernel(top, low, residual, weight, down, stream, middle, buffer, sems):
    fetch = Fetch(weight, buffer, sems, 0)
    first = []
    for i in range(2):
        row = iota((256, 512), 0) + i * 256
        order = ((row & 127) * 4 + (row >> 7) == iota((256, 512), 1)).astype(F32).astype(BF16)
        first.append(dot(order, residual[...], ((1,), (0,))))
    d = down_rows(down, 0)
    middle[:, 0:256] = dot(d, top[...], ((1,), (1,)))
    middle[:, 256:512] = dot(d, low[...], ((1,), (1,)))
    out = forward_dot([top, low], fetch, first)
    stream[0:256, :] = out[0]
    stream[256:512, :] = out[1]


def sides_kernel(
    left_top, left_low, right_top, right_low, before, middle_before, weight, down,
    stream, middle, buffer, buffer2, sems, sems2,
):
    fetch = Fetch(weight, buffer, sems, 3)
    fetch2 = Fetch(weight, buffer2, sems2, 1)
    d, d2 = down_rows(down, 3), down_rows(down, 1)
    middle[:, 0:256] = (
        middle_before[:, 0:256]
        + dot(d, left_top[...], ((1,), (1,)))
        + dot(d2, right_top[...], ((1,), (1,)))
    )
    middle[:, 256:512] = (
        middle_before[:, 256:512]
        + dot(d, left_low[...], ((1,), (1,)))
        + dot(d2, right_low[...], ((1,), (1,)))
    )
    out = forward_dot([left_top, left_low], fetch, [before[0:256, :], before[256:512, :]])
    out = forward_dot([right_top, right_low], fetch2, out)
    stream[0:256, :] = out[0]
    stream[256:512, :] = out[1]


def listed_onehot(meta):
    return (iota((128, 1024), 0).astype(F32) == meta[32:33, :]) & (meta[34:35, :] > 0.0)


def far_kernel(
    far_top, far_low, before_in, middle_before, weight, down, up, gain,
    stream_out, middle, tokens, table_out, buffer, sems, stream, out_sems, before, in_sems,
):
    fetch = Fetch(weight, buffer, sems, 2)
    arriving = [move(before_in, before, in_sems, s) for s in range(4)]
    d = down_rows(down, 2)
    mid = [
        (middle_before[:, i * 256 : i * 256 + 256] + dot(d, far[...], ((1,), (1,)))).astype(BF16)
        for i, far in enumerate((far_top, far_low))
    ]
    out = [2.0 * dot(mid[i], up[...], ((0,), (0,))) for i in range(2)]
    middle[:, 0:256] = mid[0]
    middle[:, 256:512] = mid[1]
    out = forward_dot([far_top, far_low], fetch, out)
    g = gain[...]
    columns = []
    scaled = []
    sent = []
    for s in range(4):
        arriving[s].wait()
        x = out[s // 2][(s % 2) * 128 : (s % 2) * 128 + 128] + before[s * 128 : s * 128 + 128, :]
        stream[s * 128 : s * 128 + 128, :] = x
        sent.append(move(stream, stream_out, out_sems, s))
        u = x * g
        scaled.append(u)
        columns.append(jnp.sum(x * x, axis=1, keepdims=True))
        tokens[s * 128 : s * 128 + 128, :] = u.astype(BF16)
    for a, b in PAIRS:
        columns.append(jnp.sum(scaled[a] * scaled[b], axis=1, keepdims=True))
    lane = iota((128, 128), 1)
    table = jnp.zeros((128, 128), F32)
    for place, column in enumerate(columns):
        table = jnp.where(lane == place, column, table)
    table_out[...] = table.T[0:16]
    for copy in sent:
        copy.wait()


def partial_kernel(tokens, turned, qown, meta, table, pack):
    onehot = listed_onehot(meta)
    batch = dot(qown[...], tokens[...], ((1,), (1,)))
    pack[0:16, 0:512] = batch[0:16]
    pack[0:16, 512:1024] = batch[16:32]
    for j in range(4):
        lanes = slice(j * 256, j * 256 + 256)
        scores = dot(tokens[...], turned[:, lanes], ((1,), (0,)))
        for s in range(4):
            pack[16 + s : 17 + s, lanes] = jnp.sum(
                jnp.where(onehot[:, lanes], scores[s * 128 : s * 128 + 128], 0.0),
                axis=0,
                keepdims=True,
            )
    pack[20:21, :] = meta[35:36, :]
    pack[21:23, :] = jnp.zeros((2, 1024), F32)
    for place in range(4 + len(PAIRS)):
        row, off = 21 + place // 8, (place % 8) * 128
        pack[row : row + 1, off : off + 128] = table[place : place + 1, :]
    q = qown[...].astype(F32)
    squares = jnp.sum(q * q, axis=1, keepdims=True)
    pack[23:24, 0:128] = jnp.sum(
        jnp.where(iota((32, 128), 0) == iota((32, 128), 1), squares, 0.0), axis=0, keepdims=True
    )
    pack[23:24, 128:1024] = jnp.zeros((1, 896), F32)


def score_kernel(p0, p1, p2, p3, meta, lens, slot, batch, stats, sums):
    def total(rows, lanes):
        return (p0[rows, lanes] + p2[rows, lanes]) + (p1[rows, lanes] + p3[rows, lanes])

    def stat(place):
        row, off = 21 + place // 8, (place % 8) * 128
        return total(slice(row, row + 1), slice(off, off + 128))

    every = slice(0, 1024)
    used = meta[34:35, :] > 0.0
    length = lens[...].astype(F32)
    inv = [lax.rsqrt(stat(s) / 4096.0 + 1e-05) for s in range(4)]
    a = [jnp.where(s < length, inv[s] / length, 0.0) for s in range(4)]
    gram = {pair: stat(4 + i) for i, pair in enumerate(PAIRS)}
    toward = [
        sum(a[t] * gram[(min(s, t), max(s, t))] for t in range(4)) for s in range(4)
    ]
    square = sum(a[s] * toward[s] for s in range(4))
    pinv = lax.rsqrt(square + 1e-06)
    rows = []
    for row in a + [pinv]:
        rows += split3(row)
    onehot = jnp.where(listed_onehot(meta), 1.0, 0.0).astype(BF16)
    picked = dot(stack_rows(rows, 16).astype(BF16), onehot, ((1,), (0,)))
    pick = [
        picked[3 * i : 3 * i + 1] + picked[3 * i + 1 : 3 * i + 2] + picked[3 * i + 2 : 3 * i + 3]
        for i in range(5)
    ]
    dots = [total(slice(16 + s, 17 + s), every) for s in range(4)]
    product = pick[0] * dots[0] + pick[1] * dots[1] + pick[2] * dots[2] + pick[3] * dots[3]
    qinv = lax.rsqrt(total(slice(20, 21), every) + 1e-06)
    pre = qinv * pick[4] * INV_TEMPER
    score = product * pre
    grown = jnp.where(used, jnp.exp(score), 0.0)
    slot[0:1, :] = score
    slot[1:2, :] = pre
    for s in range(4):
        slot[2 + s : 3 + s, :] = dots[s]
    slot[6:8, :] = jnp.zeros((2, 1024), F32)

    own = total(slice(23, 24), slice(0, 128))
    lane = iota((32, 128), 1)
    qcol = lax.rsqrt(
        jnp.sum(jnp.where(lane == iota((32, 128), 0), own, 0.0), axis=1, keepdims=True) + 1e-06
    )
    pieces = []
    for s in range(4):
        top = total(slice(0, 16), slice(s * 128, s * 128 + 128))
        low = total(slice(0, 16), slice(512 + s * 128, 640 + s * 128))
        pieces.append(jnp.concatenate([top, low], axis=0))
        batch[:, 256 + s * 128 : 384 + s * 128] = pieces[s]
    bpre = qcol * pinv * INV_TEMPER
    bscore = sum(a[s] * pieces[s] for s in range(4)) * bpre
    bgrown = jnp.exp(bscore)
    batch[:, 0:128] = bscore
    batch[:, 128:256] = bpre
    batch[:, 768:896] = jnp.broadcast_to(qcol, (32, 128))

    stats[...] = stack_rows(a + inv + toward + [pinv], 16)

    mine = meta[0:32, :]
    block = ((iota((1024, 128), 0) >> 5) == iota((1024, 128), 1)).astype(F32).astype(BF16)

    def by_query(row):
        out = jnp.zeros((32, 128), F32)
        for part in split3(row):
            out += dot((mine * part).astype(BF16), block, ((1,), (0,)))
        return out

    at_home = lane == lax.axis_index("dp")
    exp_sum = by_query(grown) + jnp.where(at_home, jnp.sum(bgrown, axis=1, keepdims=True), 0.0)
    place = ((iota((128, 1024), 1) & 31) == iota((128, 1024), 0)).astype(F32).astype(BF16)
    wide = jnp.zeros((32, 1024), F32)
    for part in split3(exp_sum):
        wide += dot(part.astype(BF16), place, ((1,), (0,)))
    spread = iota((32, 1024), 0) == (iota((32, 1024), 1) >> 5)
    exp_row = jnp.sum(jnp.where(spread, wide, 0.0), axis=0, keepdims=True)
    for b in range(32):
        group = slice(b // 4 * 128, b // 4 * 128 + 128)
        sums[b, :, 0:1024] = exp_row
        sums[b, :, 1024:1152] = score[:, group]
        sums[b, :, 1152:1280] = pre[:, group]


def pooled_kernel(stream_in, stats, gain, qslot, pooled, rows, stream, sems):
    for copy in [move(stream_in, stream, sems, s) for s in range(4)]:
        copy.wait()
    cols = jnp.concatenate([stats[...], jnp.zeros((112, 128), F32)], axis=0).T
    g = gain[...]
    mean = sum(cols[:, s : s + 1] * (stream[s * 128 : s * 128 + 128, :] * g) for s in range(4))
    pooled[...] = mean.astype(BF16)
    meta = qslot[:, 1024:1152].astype(F32)
    lane = iota((1024, 128), 1).astype(F32)
    listed = ((meta[:, 32:33] == lane) & (meta[:, 34:35] > 0.0)).astype(F32).astype(BF16)
    full = dot(listed, pooled[...], ((1,), (0,)))
    last = dot(last_slots(), listed, ((1,), (0,))).astype(BF16)
    fold([full], dot(last, pooled[...], ((1,), (0,))).astype(BF16), rows)


def gradient_kernel(
    recv, stream_in, qslot, qown, gain, meta, slot, batch, stats, pooled, up, middle, weight,
    grad_out, far_top, far_low, lora, extras_out, up_part,
    buffer, sems, stream, in_sems, grad, out_sems, extras, extras_sem, ordered,
):
    arriving = [move(stream_in, stream, in_sems, s) for s in range(4)]
    fetch = Fetch(weight, buffer, sems, 2)
    total = recv[0, :, 0:1024]
    for b in range(1, 32):
        total = total + recv[b, :, 0:1024]
    log_row = jnp.log(total)
    spread = iota((32, 1024), 0) == (iota((32, 1024), 1) >> 5)
    place = ((iota((1024, 128), 0) & 31) == iota((1024, 128), 1)).astype(F32).astype(BF16)
    table = jnp.zeros((32, 128), F32)
    for part in split3(log_row):
        table += dot(jnp.where(spread, part, 0.0).astype(BF16), place, ((1,), (0,)))
    block = (iota((128, 1024), 0) == (iota((128, 1024), 1) >> 5)).astype(F32).astype(BF16)
    wide = jnp.zeros((32, 1024), F32)
    for part in split3(table):
        wide += dot(part.astype(BF16), block, ((1,), (0,)))
    log_slot = jnp.sum(meta[0:32, :] * wide, axis=0, keepdims=True)
    lane = iota((32, 128), 1)
    log_col = jnp.sum(
        jnp.where(lane == lax.axis_index("dp"), table, 0.0), axis=1, keepdims=True
    )
    extras[:, 0:128] = jnp.broadcast_to(log_col, (32, 128))
    used, first = meta[34:35, :] > 0.0, meta[33:34, :]
    score = slot[0:1, :]
    coef = jnp.where(used, LOSS_SCALE * (jnp.exp(score - log_slot) - first), 0.0)
    value = (coef * slot[1:2, :]).astype(BF16).astype(F32)
    bscore = batch[:, 0:128]
    bcoef = LOSS_SCALE * jnp.exp(bscore - log_col)
    bweight = (bcoef * batch[:, 128:256]).astype(BF16).astype(F32)
    extras[:, 128:256] = bweight
    extras[:, 256:384] = bcoef * bscore
    extras_copy = pltpu.make_async_copy(extras, extras_out, extras_sem.at[0])
    extras_copy.start()
    onehot = listed_onehot(meta)
    spread_weight = jnp.where(onehot, value, 0.0)
    wb = spread_weight.astype(BF16)
    scalar = jnp.sum(jnp.where(onehot, coef * score, 0.0), axis=1, keepdims=True)

    rows = [jnp.sum(bcoef * bscore, axis=0, keepdims=True)]
    for s in range(4):
        rows.append(
            jnp.sum(bweight * batch[:, 256 + s * 128 : 384 + s * 128], axis=0, keepdims=True)
        )
    rows += [stats[i : i + 1, :] for i in range(13)]
    cols = stack_rows(rows, 128).T

    def col(i):
        return cols[:, i : i + 1]

    pinv = col(17)
    scale = (scalar + col(0)) * pinv * pinv
    g = gain[...]
    gp = dot(wb, qslot[:, 0:1024], ((1,), (0,)))
    bt = jnp.concatenate([bweight, jnp.zeros((96, 128), F32)], axis=0).T.astype(BF16)
    qpad = jnp.concatenate([qown[...], jnp.zeros((96, 1024), BF16)], axis=0)
    gp = gp + dot(bt, qpad, ((1,), (0,))) - scale * pooled[...].astype(F32)
    gg = gp * g
    leaving = [extras_copy]
    for s in range(4):
        arriving[s].wait()
        x = stream[s * 128 : s * 128 + 128, :]
        a, inv = col(5 + s), col(9 + s)
        inner = (
            jnp.sum(spread_weight * slot[2 + s : 3 + s, :], axis=1, keepdims=True)
            + col(1 + s)
            - scale * col(13 + s)
        )
        beta = inv * inv * a * inner / 4096.0
        ordered[s * 128 : s * 128 + 128, :] = (a * gg - beta * x).astype(BF16)
    token = iota((512, 512), 0)
    order = ((token & 3) * 128 + (token >> 2) == iota((512, 512), 1)).astype(F32).astype(BF16)
    grad[...] = dot(order, ordered[...], ((1,), (0,))).astype(BF16)
    leaving += [move(grad, grad_out, out_sems, s) for s in range(4)]
    lora[...] = dot(up[...], grad[...], ((1,), (1,)))
    up_part[...] = dot(middle[...], ordered[...], ((1,), (0,)))
    for k in range(4):
        fetch.wait(k)
        for i, out in enumerate((far_top, far_low)):
            out[:, k * 256 : k * 256 + 256] = dot(
                grad[i * 256 : i * 256 + 256, :], buffer[k * 256 : k * 256 + 256, :], ((1,), (1,))
            ).astype(BF16)
    for copy in leaving:
        copy.wait()


def sides_back_kernel(
    grad_in, weight,
    right_low, left_top, right_top, left_low,
    buffer, buffer2, sems, sems2, grad, in_sems,
):
    arriving = [move(grad_in, grad, in_sems, s) for s in range(4)]
    fetch = Fetch(weight, buffer, sems, 1)
    fetch2 = Fetch(weight, buffer2, sems2, 3)
    for copy in arriving:
        copy.wait()
    for fetched, low, top in ((fetch, right_low, right_top), (fetch2, left_low, left_top)):
        for k in range(4):
            fetched.wait(k)
            part = fetched.buffer[k * 256 : k * 256 + 256, :]
            columns = slice(k * 256, k * 256 + 256)
            top[:, columns] = dot(grad[0:256, :], part, ((1,), (1,))).astype(top.dtype)
            low[:, columns] = dot(grad[256:512, :], part, ((1,), (1,))).astype(low.dtype)


def join_kernel(l0, l1, l2, l3, tokens, up_part, adapter, lora_back):
    lora = (2.0 * ((l0[...] + l2[...]) + (l1[...] + l3[...]))).astype(BF16)
    lora_back[...] = lora
    adapter[0:16, :] = dot(lora, tokens[...], ((1,), (0,))).astype(BF16)
    adapter[16:32, :] = up_part[...].astype(BF16)


def add_kernel(right_top, left_low, via_right, via_left, to_right, to_left):
    to_right[...] = (right_top[...].astype(F32) + via_right[...].astype(F32)).astype(BF16)
    to_left[...] = (left_low[...].astype(F32) + via_left[...].astype(F32)).astype(BF16)


def pair_kernel(a, b, out):
    out[...] = (a[...].astype(F32) + b[...].astype(F32)).astype(BF16)


def four_sum(parts):
    a, b, c, d = [part[...].astype(F32) for part in parts]
    return (a + c) + (b + d)


def four_kernel(a, b, c, d, out):
    out[...] = four_sum((a, b, c, d)).astype(BF16)


def last_kernel(a, b, c, d, down, up):
    total = four_sum((a, b, c, d))
    down[...] = total[0:16]
    up[...] = 2.0 * total[16:32]


def finish_kernel(before, from_left, from_right, out):
    out[0:256, :] = (before[0:256, :] + from_left[...].astype(F32)).astype(BF16)
    out[256:512, :] = (before[256:512, :] + from_right[...].astype(F32)).astype(BF16)


def own_back_kernel(
    grad_in, weight, down, lora_back, from_right, from_left, out, buffer, sems, grad, in_sems
):
    arriving = [move(grad_in, grad, in_sems, s) for s in range(4)]
    fetch = Fetch(weight, buffer, sems, 0)
    local = dot(lora_back[...], down_rows(down, 0), ((0,), (0,)))
    for copy in arriving:
        copy.wait()
    for k in range(4):
        fetch.wait(k)
        lanes = slice(k * 256, k * 256 + 256)
        own = local[:, lanes] + dot(grad[...], buffer[k * 256 : k * 256 + 256, :], ((1,), (1,)))
        out[0:256, lanes] = own[0:256] + from_right[:, lanes].astype(F32)
        out[256:512, lanes] = own[256:512] + from_left[:, lanes].astype(F32)


def query_kernel(
    recv, home, extras, batch, pooled, qown, arrived, gradient, loss, listed
):
    group = lax.rem(lax.axis_index("dp"), 4) * 32
    place = iota((128, 1024), 0) == (iota((128, 1024), 1) & 31) + group
    place = place.astype(F32).astype(BF16)
    spread = iota((32, 1024), 0) == (iota((32, 1024), 1) >> 5)
    sub = iota((32, 128), 0)

    def by_slot(lanes):
        table = jnp.zeros((32, 128), F32)
        for d in range(32):
            table = jnp.where(sub == d, recv[d, :, lanes], table)
        wide = jnp.zeros((32, 1024), F32)
        for part in split3(table):
            wide += dot(part.astype(BF16), place, ((1,), (0,)))
        return jnp.sum(jnp.where(spread, wide, 0.0), axis=0, keepdims=True)

    score, pre = by_slot(slice(1024, 1152)), by_slot(slice(1152, 1280))
    mine, first, used = home[0:32, :], home[33:34, :], home[34:35, :] > 0.0
    log_col = extras[:, 0:1]
    log_slot = jnp.sum(mine * log_col, axis=0, keepdims=True)
    coef = jnp.where(used, LOSS_SCALE * (jnp.exp(score - log_slot) - first), 0.0)
    value = jnp.where(used, coef * pre, 0.0).astype(BF16).astype(F32)
    score = jnp.where(used, score, 0.0)
    positive = jnp.sum(mine * (first * score), axis=1, keepdims=True)
    scalar = jnp.sum(mine * (coef * score), axis=1, keepdims=True)
    scalar = scalar + jnp.sum(extras[:, 256:384], axis=1, keepdims=True)
    eye = iota((32, 128), 0) == iota((32, 128), 1)
    row = jnp.sum(jnp.where(eye, log_col - positive, 0.0), axis=0, keepdims=True)
    loss[...] = row[:, 0:32]
    qinv = batch[:, 768:769]
    unfold(arrived, listed)
    total = dot((mine * value).astype(BF16), listed[...], ((1,), (0,)))
    total = total + dot(extras[:, 128:256].astype(BF16), pooled[...], ((1,), (0,)))
    gradient[...] = (total - (scalar * qinv * qinv) * qown[...].astype(F32)).astype(BF16)


ANY, HOLD, LOAD, STORE = "any", "hold", "load", "store"


def call(kernel, outs, args, scratch=(), limit=16, cost=None):
    in_specs, values, moved = [], [], []
    for place, arg in enumerate(args):
        space = pltpu.VMEM
        if isinstance(arg, tuple):
            arg, mark = arg
            space = pltpu.HBM
            if mark != ANY:
                arg = pltpu.with_memory_space_constraint(arg, pltpu.HBM)
            if mark == LOAD:
                moved.append((place, arg.shape, arg.dtype))
        values.append(arg)
        in_specs.append(pl.BlockSpec(memory_space=space))
    loads = len(moved)
    for place, (shape, dtype, *mark) in enumerate(outs):
        if mark == [STORE]:
            moved.append((len(args) + place, shape, dtype))
    count, extra = len(args) + len(outs), len(moved)

    def whole(*refs):
        refs = list(refs)
        if not extra:
            return kernel(*refs)
        sems = refs.pop()
        buffers = [refs.pop() for _ in range(extra)][::-1]
        copies = []
        for i, (place, _, _) in enumerate(moved):
            ends = (refs[place], buffers[i]) if i < loads else (buffers[i], refs[place])
            copies.append(pltpu.make_async_copy(*ends, sems.at[i]))
            refs[place] = buffers[i]
        for copy in copies[:loads]:
            copy.start()
        for copy in copies[:loads]:
            copy.wait()
        kernel(*refs)
        for copy in copies[loads:]:
            copy.start()
        for copy in copies[loads:]:
            copy.wait()

    scratch = list(scratch)
    if extra:
        scratch += [pltpu.VMEM(shape, dtype) for _, shape, dtype in moved]
        scratch.append(pltpu.SemaphoreType.DMA((extra,)))
    if cost is not None:
        cost = pl.CostEstimate(flops=int(cost * 1.15e9), bytes_accessed=0, transcendentals=0)
    return pl.pallas_call(
        whole,
        cost_estimate=cost,
        name=kernel.__name__,
        out_shape=[
            (pltpu.HBM if mark else jax.ShapeDtypeStruct)(s, t) for s, t, *mark in outs
        ],
        in_specs=in_specs,
        out_specs=[
            pl.BlockSpec(memory_space=pltpu.HBM if mark else pltpu.VMEM) for _, _, *mark in outs
        ],
        scratch_shapes=scratch,
        compiler_params=pltpu.CompilerParams(vmem_limit_bytes=limit * 2**20),
    )(*values)


COST_OWN = 15.0
COST_PAIR = 3.0
COST_JOIN = 16.0
COST_GRAD = 1.0
COST_FAR = 4.0
COST_SIDES = 1.0
WEIGHT_BUFFER = pltpu.VMEM((1024, 1024), BF16)
FOUR = pltpu.SemaphoreType.DMA((4,))


def ring(x, step):
    return lax.ppermute(x, "mp", [(i, (i + step) % 4) for i in range(4)])


def ring_sum(x):
    return (x + ring(x, 2)) + (ring(x, 1) + ring(x, 3))


def grid_index(x, y, core):
    return (x * 4 + y) * 2 + core


def grid_shift(v, axis, step):
    pairs = []
    for x in range(4):
        for y in range(4):
            for core in range(2):
                if axis == "core":
                    to = (x, y, 1 - core)
                elif axis == "x":
                    to = ((x + step) % 4, y, core)
                else:
                    to = (x, (y + step) % 4, core)
                pairs.append((grid_index(x, y, core), grid_index(*to)))
    return lax.ppermute(v, "dp", pairs)


def grid_sum(x, own, query):
    shape = x.shape
    tie = lax.optimization_barrier
    (x,) = call(pair_kernel, [(shape, BF16)], [x, grid_shift(x, "core", 1)], cost=COST_PAIR)
    parts = [x] + [grid_shift(x, "x", step) for step in (1, 2, 3)]
    own, *parts = tie((own, *parts))
    (x,) = call(four_kernel, [(shape, BF16)], parts)
    parts = [x] + [grid_shift(x, "y", step) for step in (1, 2, 3)]
    query, own, *parts = tie((query, own, *parts))
    down, up = call(last_kernel, [((16, 1024), F32), ((16, 1024), F32)], parts)
    return down, up, own, query


def body(
    attention_output,
    residual,
    output_projection_weight,
    adapter_down_matrix,
    adapter_up_matrix,
    final_norm_gain,
    query_hidden_states,
    pair_passage_index,
    lengths,
):
    weight = (output_projection_weight, HOLD)
    down = adapter_down_matrix.T
    up = adapter_up_matrix
    qown = query_hidden_states
    half, full = (256, 1024), (512, 1024)
    tie = lax.optimization_barrier

    top, low = call(
        order_kernel, [(half, BF16), (half, BF16)], [(attention_output, LOAD)]
    )
    with jax.named_scope("leg1"):
        left_top, right_low = ring(top, 1), ring(low, 3)

    ids, _, _ = tie((pair_passage_index, top, low))
    flat = jnp.pad(ids.reshape(-1), (0, 640 - 544), constant_values=-1)
    qslot_out, home = call(
        slot_kernel,
        [((768, 1280), BF16, STORE), ((40, 1024), F32, STORE)],
        [flat.reshape(1, 640), flat.reshape(640, 1), qown],
    )
    with jax.named_scope("a2a_queries"):
        qslot = lax.all_to_all(qslot_out, "dp", 0, 0, tiled=True)
    with jax.named_scope("leg2"):
        left_low, right_top = ring(low, 1), ring(top, 3)
    with jax.named_scope("leg3"):
        far_top, far_low = ring(left_top, 1), ring(right_low, 3)

    residual_tied, left_top, right_low = tie((residual, left_top, right_low))
    stream, middle = call(
        own_kernel,
        [(full, F32), ((16, 512), F32)],
        [top, low, residual_tied, weight, down],
        [WEIGHT_BUFFER, FOUR], limit=24, cost=COST_OWN,
    )
    stream, middle = call(
        sides_kernel,
        [(full, F32, STORE), ((16, 512), F32)],
        [left_top, left_low, right_top, right_low, stream, middle, weight, down],
        [WEIGHT_BUFFER, WEIGHT_BUFFER, FOUR, FOUR], limit=24,
    )
    gain = final_norm_gain.astype(F32).reshape(1, 1024)
    stream, middle, tokens, table = call(
        far_kernel,
        [(full, F32, ANY), ((16, 512), BF16), (full, BF16), ((16, 128), F32)],
        [far_top, far_low, (stream, HOLD), middle, weight, down, up, gain],
        [WEIGHT_BUFFER, FOUR, pltpu.VMEM(full, F32), FOUR, pltpu.VMEM(full, F32), FOUR],
        limit=24,
        cost=COST_FAR,
    )
    qslot, table = tie((qslot, table))
    qslot, meta, turned = call(
        meta_kernel,
        [((1024, 1152), BF16), ((40, 1024), F32), ((1024, 1024), BF16)],
        [(qslot, LOAD)],
    )
    (pack,) = call(partial_kernel, [((24, 1024), F32)], [tokens, turned, qown, meta, table])
    with jax.named_scope("packs"):
        packs = [pack, ring(pack, 1), ring(pack, 2), ring(pack, 3)]
    slot, batch, stats, sums = call(
        score_kernel,
        [((8, 1024), F32), ((32, 896), F32), ((16, 128), F32), ((32, 1, 1280), F32)],
        [*packs, meta, lengths.reshape(1, 128)],
    )
    with jax.named_scope("a2a_sums"):
        recv = lax.all_to_all(sums, "dp", 0, 0, tiled=True)
    pooled, rows = call(
        pooled_kernel,
        [((128, 1024), BF16), ((768, 1152), BF16)],
        [(stream, HOLD), stats, gain, qslot],
        [pltpu.VMEM(full, F32), FOUR],
    )
    grad, far_top, far_low, lora, extras, up_part = call(
        gradient_kernel,
        [
            (full, BF16, ANY), (half, BF16), (half, BF16), ((16, 512), F32),
            ((32, 384), F32, ANY), ((16, 1024), F32),
        ],
        [recv, (stream, HOLD), qslot, qown, gain, meta, slot, batch, stats, pooled, up, middle, weight],
        [
            WEIGHT_BUFFER, FOUR, pltpu.VMEM(full, F32), FOUR, pltpu.VMEM(full, BF16), FOUR,
            pltpu.VMEM((32, 384), F32), pltpu.SemaphoreType.DMA((1,)), pltpu.VMEM(full, BF16),
        ],
        limit=24, cost=COST_GRAD,
    )

    far_top, far_low, rows = tie((far_top, far_low, rows))
    with jax.named_scope("back1"):
        via_right, via_left = ring(far_top, 1), ring(far_low, 3)
    with jax.named_scope("lora_sum"):
        loras = [lora, ring(lora, 1), ring(lora, 2), ring(lora, 3)]
    with jax.named_scope("a2a_rows"):
        arrived = lax.all_to_all(rows, "dp", 0, 0, tiled=True)
    right_low, left_top, right_top, left_low = call(
        sides_back_kernel,
        [(half, BF16), (half, BF16), (half, BF16), (half, BF16)],
        [(grad, ANY), weight],
        [WEIGHT_BUFFER, WEIGHT_BUFFER, FOUR, FOUR, pltpu.VMEM(full, BF16), FOUR],
        limit=24,
        cost=COST_SIDES,
    )
    with jax.named_scope("back2"):
        to_right_low, to_left_top = ring(right_low, 1), ring(left_top, 3)
    right_top, left_low = call(
        add_kernel,
        [(half, BF16), (half, BF16)],
        [right_top, left_low, via_right, via_left],
    )
    right_top, left_low, up_part = tie((right_top, left_low, up_part))
    adapter, lora_back = call(
        join_kernel,
        [((32, 1024), BF16), ((16, 512), BF16)],
        [*loras, (attention_output, LOAD), up_part],
        cost=COST_JOIN,
    )
    with jax.named_scope("back3"):
        to_right_top, to_left_low = ring(right_top, 1), ring(left_low, 3)
    (before,) = call(
        own_back_kernel,
        [(full, F32)],
        [(grad, ANY), weight, down, lora_back, to_left_top, to_right_low],
        [WEIGHT_BUFFER, FOUR, pltpu.VMEM(full, BF16), FOUR],
        limit=24,
    )
    query_gradient, loss = call(
        query_kernel,
        [((32, 1024), BF16), ((1, 32), F32)],
        [
            (recv, LOAD), (home, LOAD), (extras, LOAD), (batch, LOAD), (pooled, LOAD),
            (qown, LOAD), arrived,
        ],
        [pltpu.VMEM((1024, 1024), BF16)],
    )
    with jax.named_scope("adapters"):
        down_grad, up_grad, before, query_gradient = grid_sum(adapter, before, query_gradient)
    (attention_gradient,) = call(
        finish_kernel,
        [(full, BF16)],
        [before, to_right_top, to_left_low],
    )
    return (
        loss.reshape(32),
        query_gradient,
        grad,
        attention_gradient,
        down_grad.T,
        up_grad,
    )


def solution(mesh):
    in_specs = (
        P("dp", "mp"),
        P("dp", "mp"),
        P(None, "mp"),
        P(),
        P(None, "mp"),
        P("mp"),
        P("dp", "mp"),
        P("dp", None),
        P("dp"),
    )
    out_specs = (P("dp"), P("dp", "mp"), P("dp", "mp"), P("dp", "mp"), P("mp", None), P(None, "mp"))
    return jax.shard_map(body, mesh=mesh, in_specs=in_specs, out_specs=out_specs, check_vma=False)
```

```python
import jax
import jax.numpy as jnp
from jax import lax
from jax.experimental import pallas as pl
from jax.experimental.pallas import tpu as pltpu
from jax.sharding import PartitionSpec as P

F32 = jnp.float32
BF16 = jnp.bfloat16
INV_TEMPER = 1.0 / 0.02
LOSS_SCALE = 1024.0
SLOTS = 32
HARD = 17
PAIRS = [(a, b) for a in range(4) for b in range(a, 4)]


def dot(a, b, dims):
    return lax.dot_general(a, b, ((dims[0], dims[1]), ((), ())), preferred_element_type=F32)


def split3(x):
    a = x.astype(BF16).astype(F32)
    b = (x - a).astype(BF16).astype(F32)
    return [a, b, x - a - b]


def iota(shape, dim):
    return lax.broadcasted_iota(jnp.int32, shape, dim)


def stack_rows(rows, height):
    where = iota((height, rows[0].shape[1]), 0)
    total = jnp.zeros((height, rows[0].shape[1]), F32)
    for place, row in enumerate(rows):
        total = jnp.where(where == place, row, total)
    return total


def step_of(offset):
    return lax.rem(lax.axis_index("mp") + offset, 4)


class Fetch:
    def __init__(self, weight, buffer, sems, offset):
        base = step_of(offset) * 1024
        self.buffer = buffer
        self.copies = [
            pltpu.make_async_copy(
                weight.at[pl.ds(pl.multiple_of(base + k * 256, 256), 256), :],
                buffer.at[pl.ds(k * 256, 256), :],
                sems.at[k],
            )
            for k in range(4)
        ]
        for copy in self.copies:
            copy.start()

    def wait(self, k):
        self.copies[k].wait()


def move(source, target, sems, part):
    rows = pl.ds(part * 128, 128)
    copy = pltpu.make_async_copy(source.at[rows, :], target.at[rows, :], sems.at[part])
    copy.start()
    return copy


def down_rows(down, offset):
    return down[:, pl.ds(pl.multiple_of(step_of(offset) * 1024, 1024), 1024)]


def forward_dot(blocks, fetch, first):
    out = list(first)
    for k in range(4):
        fetch.wait(k)
        part = fetch.buffer[k * 256 : k * 256 + 256, :]
        for i, block in enumerate(blocks):
            out[i] = out[i] + dot(block[:, k * 256 : k * 256 + 256], part, ((1,), (0,)))
    return out


def order_kernel(tokens, top, low):
    for i, out in enumerate((top, low)):
        row = iota((256, 512), 0) + i * 256
        order = ((row & 127) * 4 + (row >> 7) == iota((256, 512), 1)).astype(F32).astype(BF16)
        out[...] = dot(order, tokens[...], ((1,), (0,))).astype(BF16)


def fold_map(shape, slot_dim):
    part = iota(shape, 1 - slot_dim)
    return iota(shape, slot_dim) == (part & 31) * 24 + (part >> 5)


def fold(pieces, last, out):
    width = last.shape[1]
    off = 0
    for piece in pieces:
        lanes = slice(off, off + piece.shape[1])
        kept = [piece[o * 32 : o * 32 + 24] for o in range(32)]
        out[:, lanes] = jnp.concatenate(kept, axis=0).astype(BF16)
        off += piece.shape[1]
    stack = jnp.concatenate([last[:, i : i + 128] for i in range(0, width, 128)], axis=0)
    table = fold_map((768, stack.shape[0]), 0).astype(F32).astype(BF16)
    out[:, width : width + 128] = dot(table, stack, ((1,), (0,))).astype(BF16)


def last_rows(extra, width):
    parts = width // 128
    table = fold_map((parts * 32, 768), 1).astype(F32).astype(BF16)
    stack = dot(table, extra, ((1,), (0,)))
    last = jnp.concatenate([stack[c * 32 : c * 32 + 32] for c in range(parts)], axis=1)
    last = jnp.concatenate([last, jnp.zeros((96, width), F32)], axis=0).astype(BF16)
    place = (iota((256, 128), 0) == iota((256, 128), 1) * 8).astype(F32).astype(BF16)
    return dot(place, last, ((1,), (0,)))


def unfold(kept, last, first):
    pieces = []
    for i in range(8):
        pieces.append(kept[i * 24 : i * 24 + 24])
        pieces.append(last[(first + i) * 8 : (first + i) * 8 + 8])
    return jnp.concatenate(pieces, axis=0)


def last_slots():
    return (iota((32, 1024), 1) == iota((32, 1024), 0) * 32 + 24).astype(F32).astype(BF16)


def slot_kernel(ids_row, ids_col, queries, out, home):
    ids = ids_row[...]
    owner = iota((32, 640), 0)
    owned = (ids >> 7) == owner
    before = (iota((640, 640), 0) < iota((640, 640), 1)).astype(F32).astype(BF16)
    rank = dot(owned.astype(F32).astype(BF16), before, ((1,), (0,)))
    slot = jnp.sum(jnp.where(owned, rank + (owner * SLOTS).astype(F32), 0.0), axis=0, keepdims=True)
    slot = jnp.where(ids < 0, -1.0, slot).astype(jnp.int32)
    listed = (iota((1024, 640), 0) == slot).astype(F32).astype(BF16)
    entry, lane = iota((640, 128), 0), iota((640, 128), 1)
    query = (entry * 241) >> 12
    values = jnp.where(lane < 32, (query == lane).astype(F32), 0.0)
    values = jnp.where(lane == 32, (ids_col[...] & 127).astype(F32), values)
    values = jnp.where((lane == 33) & (query * HARD == entry), 1.0, values)
    values = jnp.where(lane == 34, 1.0, values)
    picked = dot(listed, values.astype(BF16), ((1,), (0,)))
    q = queries[...].astype(F32)
    squares = jnp.sum(q * q, axis=1, keepdims=True)
    square_row = jnp.sum(
        jnp.where(iota((32, 128), 0) == iota((32, 128), 1), squares, 0.0), axis=0, keepdims=True
    )
    lane = iota((1024, 128), 1)
    mine = jnp.where(lane < 32, picked, 0.0)
    square = jnp.sum(mine * square_row, axis=1, keepdims=True)
    for i, part in enumerate(split3(square)):
        picked = jnp.where(lane == 35 + i, part, picked)
    home[...] = picked.T[0:40, :]
    padded = jnp.concatenate([queries[...], jnp.zeros((96, 1024), BF16)], axis=0)
    rows = dot(mine.astype(BF16), padded, ((1,), (0,)))
    last = dot(last_slots(), mine.astype(BF16), ((1,), (0,))).astype(BF16)
    last = dot(last, padded, ((1,), (0,))).astype(BF16)
    last_values = dot(last_slots(), picked.astype(BF16), ((1,), (0,))).astype(BF16)
    fold([rows, picked], jnp.concatenate([last, last_values], axis=1), out)


def meta_kernel(arrived, qslot, meta, turned, main, extra, sems):
    copies = [pltpu.make_async_copy(arrived.at[:, 1152:1280], extra, sems.at[4])]
    for c in range(4):
        rows = pl.ds(c * 192, 192)
        copies.append(pltpu.make_async_copy(arrived.at[rows, 0:1152], main.at[rows, :], sems.at[c]))
    for copy in copies:
        copy.start()
    copies[0].wait()
    last = last_rows(extra[...], 1152)
    for c in range(4):
        copies[c + 1].wait()
        rows = unfold(main[c * 192 : c * 192 + 192, :].astype(F32), last, c * 8)
        lanes = slice(c * 256, c * 256 + 256)
        qslot[lanes, :] = rows.astype(BF16)
        turned[:, lanes] = rows[:, 0:1024].T.astype(BF16)
        meta[0:40, lanes] = rows[:, 1024:1152].T[0:40]
    meta[35:36, :] = meta[35:36, :] + meta[36:37, :] + meta[37:38, :]


def own_kernel(top, low, residual, weight, down, stream, middle, buffer, sems):
    fetch = Fetch(weight, buffer, sems, 0)
    first = []
    for i in range(2):
        row = iota((256, 512), 0) + i * 256
        order = ((row & 127) * 4 + (row >> 7) == iota((256, 512), 1)).astype(F32).astype(BF16)
        first.append(dot(order, residual[...], ((1,), (0,))))
    d = down_rows(down, 0)
    middle[:, 0:256] = dot(d, top[...], ((1,), (1,)))
    middle[:, 256:512] = dot(d, low[...], ((1,), (1,)))
    out = forward_dot([top, low], fetch, first)
    stream[0:256, :] = out[0]
    stream[256:512, :] = out[1]


def sides_kernel(
    left_top, left_low, right_top, right_low, before, middle_before, weight, down,
    stream, middle, buffer, buffer2, sems, sems2,
):
    fetch = Fetch(weight, buffer, sems, 3)
    fetch2 = Fetch(weight, buffer2, sems2, 1)
    d, d2 = down_rows(down, 3), down_rows(down, 1)
    middle[:, 0:256] = (
        middle_before[:, 0:256]
        + dot(d, left_top[...], ((1,), (1,)))
        + dot(d2, right_top[...], ((1,), (1,)))
    )
    middle[:, 256:512] = (
        middle_before[:, 256:512]
        + dot(d, left_low[...], ((1,), (1,)))
        + dot(d2, right_low[...], ((1,), (1,)))
    )
    out = forward_dot([left_top, left_low], fetch, [before[0:256, :], before[256:512, :]])
    out = forward_dot([right_top, right_low], fetch2, out)
    stream[0:256, :] = out[0]
    stream[256:512, :] = out[1]


def listed_onehot(meta):
    return (iota((128, 1024), 0).astype(F32) == meta[32:33, :]) & (meta[34:35, :] > 0.0)


def far_kernel(
    far_top, far_low, before_in, middle_before, weight, down, up, gain,
    stream_out, middle, tokens, table_out, buffer, sems, stream, out_sems, before, in_sems,
):
    fetch = Fetch(weight, buffer, sems, 2)
    arriving = [move(before_in, before, in_sems, s) for s in range(4)]
    d = down_rows(down, 2)
    mid = [
        (middle_before[:, i * 256 : i * 256 + 256] + dot(d, far[...], ((1,), (1,)))).astype(BF16)
        for i, far in enumerate((far_top, far_low))
    ]
    out = [2.0 * dot(mid[i], up[...], ((0,), (0,))) for i in range(2)]
    middle[:, 0:256] = mid[0]
    middle[:, 256:512] = mid[1]
    out = forward_dot([far_top, far_low], fetch, out)
    g = gain[...]
    columns = []
    scaled = []
    sent = []
    for s in range(4):
        arriving[s].wait()
        x = out[s // 2][(s % 2) * 128 : (s % 2) * 128 + 128] + before[s * 128 : s * 128 + 128, :]
        stream[s * 128 : s * 128 + 128, :] = x
        sent.append(move(stream, stream_out, out_sems, s))
        u = x * g
        scaled.append(u)
        columns.append(jnp.sum(x * x, axis=1, keepdims=True))
        tokens[s * 128 : s * 128 + 128, :] = u.astype(BF16)
    for a, b in PAIRS:
        columns.append(jnp.sum(scaled[a] * scaled[b], axis=1, keepdims=True))
    lane = iota((128, 128), 1)
    table = jnp.zeros((128, 128), F32)
    for place, column in enumerate(columns):
        table = jnp.where(lane == place, column, table)
    table_out[...] = table.T[0:16]
    for copy in sent:
        copy.wait()


def partial_kernel(tokens, turned, qown, meta, table, pack):
    onehot = listed_onehot(meta)
    batch = dot(qown[...], tokens[...], ((1,), (1,)))
    pack[0:16, 0:512] = batch[0:16]
    pack[0:16, 512:1024] = batch[16:32]
    for j in range(4):
        lanes = slice(j * 256, j * 256 + 256)
        scores = dot(tokens[...], turned[:, lanes], ((1,), (0,)))
        for s in range(4):
            pack[16 + s : 17 + s, lanes] = jnp.sum(
                jnp.where(onehot[:, lanes], scores[s * 128 : s * 128 + 128], 0.0),
                axis=0,
                keepdims=True,
            )
    pack[20:21, :] = meta[35:36, :]
    pack[21:23, :] = jnp.zeros((2, 1024), F32)
    for place in range(4 + len(PAIRS)):
        row, off = 21 + place // 8, (place % 8) * 128
        pack[row : row + 1, off : off + 128] = table[place : place + 1, :]
    q = qown[...].astype(F32)
    squares = jnp.sum(q * q, axis=1, keepdims=True)
    pack[23:24, 0:128] = jnp.sum(
        jnp.where(iota((32, 128), 0) == iota((32, 128), 1), squares, 0.0), axis=0, keepdims=True
    )
    pack[23:24, 128:1024] = jnp.zeros((1, 896), F32)


def score_kernel(p0, p1, p2, p3, meta, lens, slot, batch, stats, sums):
    def total(rows, lanes):
        return (p0[rows, lanes] + p2[rows, lanes]) + (p1[rows, lanes] + p3[rows, lanes])

    def stat(place):
        row, off = 21 + place // 8, (place % 8) * 128
        return total(slice(row, row + 1), slice(off, off + 128))

    every = slice(0, 1024)
    used = meta[34:35, :] > 0.0
    length = lens[...].astype(F32)
    inv = [lax.rsqrt(stat(s) / 4096.0 + 1e-05) for s in range(4)]
    a = [jnp.where(s < length, inv[s] / length, 0.0) for s in range(4)]
    gram = {pair: stat(4 + i) for i, pair in enumerate(PAIRS)}
    toward = [
        sum(a[t] * gram[(min(s, t), max(s, t))] for t in range(4)) for s in range(4)
    ]
    square = sum(a[s] * toward[s] for s in range(4))
    pinv = lax.rsqrt(square + 1e-06)
    rows = []
    for row in a + [pinv]:
        rows += split3(row)
    onehot = jnp.where(listed_onehot(meta), 1.0, 0.0).astype(BF16)
    picked = dot(stack_rows(rows, 16).astype(BF16), onehot, ((1,), (0,)))
    pick = [
        picked[3 * i : 3 * i + 1] + picked[3 * i + 1 : 3 * i + 2] + picked[3 * i + 2 : 3 * i + 3]
        for i in range(5)
    ]
    dots = [total(slice(16 + s, 17 + s), every) for s in range(4)]
    product = pick[0] * dots[0] + pick[1] * dots[1] + pick[2] * dots[2] + pick[3] * dots[3]
    qinv = lax.rsqrt(total(slice(20, 21), every) + 1e-06)
    pre = qinv * pick[4] * INV_TEMPER
    score = product * pre
    grown = jnp.where(used, jnp.exp(score), 0.0)
    slot[0:1, :] = score
    slot[1:2, :] = pre
    for s in range(4):
        slot[2 + s : 3 + s, :] = dots[s]
    slot[6:8, :] = jnp.zeros((2, 1024), F32)

    own = total(slice(23, 24), slice(0, 128))
    lane = iota((32, 128), 1)
    qcol = lax.rsqrt(
        jnp.sum(jnp.where(lane == iota((32, 128), 0), own, 0.0), axis=1, keepdims=True) + 1e-06
    )
    pieces = []
    for s in range(4):
        top = total(slice(0, 16), slice(s * 128, s * 128 + 128))
        low = total(slice(0, 16), slice(512 + s * 128, 640 + s * 128))
        pieces.append(jnp.concatenate([top, low], axis=0))
        batch[:, 256 + s * 128 : 384 + s * 128] = pieces[s]
    bpre = qcol * pinv * INV_TEMPER
    bscore = sum(a[s] * pieces[s] for s in range(4)) * bpre
    bgrown = jnp.exp(bscore)
    batch[:, 0:128] = bscore
    batch[:, 128:256] = bpre
    batch[:, 768:896] = jnp.broadcast_to(qcol, (32, 128))

    stats[...] = stack_rows(a + inv + toward + [pinv], 16)

    mine = meta[0:32, :]
    block = ((iota((1024, 128), 0) >> 5) == iota((1024, 128), 1)).astype(F32).astype(BF16)

    def by_query(row):
        out = jnp.zeros((32, 128), F32)
        for part in split3(row):
            out += dot((mine * part).astype(BF16), block, ((1,), (0,)))
        return out

    at_home = lane == lax.axis_index("dp")
    exp_sum = by_query(grown) + jnp.where(at_home, jnp.sum(bgrown, axis=1, keepdims=True), 0.0)
    place = ((iota((128, 1024), 1) & 31) == iota((128, 1024), 0)).astype(F32).astype(BF16)
    wide = jnp.zeros((32, 1024), F32)
    for part in split3(exp_sum):
        wide += dot(part.astype(BF16), place, ((1,), (0,)))
    spread = iota((32, 1024), 0) == (iota((32, 1024), 1) >> 5)
    exp_row = jnp.sum(jnp.where(spread, wide, 0.0), axis=0, keepdims=True)
    for b in range(32):
        group = slice(b // 4 * 128, b // 4 * 128 + 128)
        sums[b, :, 0:1024] = exp_row
        sums[b, :, 1024:1152] = score[:, group]
        sums[b, :, 1152:1280] = pre[:, group]


def pooled_kernel(stream_in, stats, gain, qslot, pooled, rows, stream, sems):
    for copy in [move(stream_in, stream, sems, s) for s in range(4)]:
        copy.wait()
    cols = jnp.concatenate([stats[...], jnp.zeros((112, 128), F32)], axis=0).T
    g = gain[...]
    mean = sum(cols[:, s : s + 1] * (stream[s * 128 : s * 128 + 128, :] * g) for s in range(4))
    pooled[...] = mean.astype(BF16)
    meta = qslot[:, 1024:1152].astype(F32)
    lane = iota((1024, 128), 1).astype(F32)
    listed = ((meta[:, 32:33] == lane) & (meta[:, 34:35] > 0.0)).astype(F32).astype(BF16)
    full = dot(listed, pooled[...], ((1,), (0,)))
    last = dot(last_slots(), listed, ((1,), (0,))).astype(BF16)
    fold([full], dot(last, pooled[...], ((1,), (0,))).astype(BF16), rows)


def gradient_kernel(
    recv, stream_in, qslot, qown, gain, meta, slot, batch, stats, pooled, up, middle, weight,
    grad_out, far_top, far_low, lora, extras_out, up_part,
    buffer, sems, stream, in_sems, grad, out_sems, extras, extras_sem, ordered,
):
    arriving = [move(stream_in, stream, in_sems, s) for s in range(4)]
    fetch = Fetch(weight, buffer, sems, 2)
    total = recv[0, :, 0:1024]
    for b in range(1, 32):
        total = total + recv[b, :, 0:1024]
    log_row = jnp.log(total)
    spread = iota((32, 1024), 0) == (iota((32, 1024), 1) >> 5)
    place = ((iota((1024, 128), 0) & 31) == iota((1024, 128), 1)).astype(F32).astype(BF16)
    table = jnp.zeros((32, 128), F32)
    for part in split3(log_row):
        table += dot(jnp.where(spread, part, 0.0).astype(BF16), place, ((1,), (0,)))
    block = (iota((128, 1024), 0) == (iota((128, 1024), 1) >> 5)).astype(F32).astype(BF16)
    wide = jnp.zeros((32, 1024), F32)
    for part in split3(table):
        wide += dot(part.astype(BF16), block, ((1,), (0,)))
    log_slot = jnp.sum(meta[0:32, :] * wide, axis=0, keepdims=True)
    lane = iota((32, 128), 1)
    log_col = jnp.sum(
        jnp.where(lane == lax.axis_index("dp"), table, 0.0), axis=1, keepdims=True
    )
    extras[:, 0:128] = jnp.broadcast_to(log_col, (32, 128))
    used, first = meta[34:35, :] > 0.0, meta[33:34, :]
    score = slot[0:1, :]
    coef = jnp.where(used, LOSS_SCALE * (jnp.exp(score - log_slot) - first), 0.0)
    value = (coef * slot[1:2, :]).astype(BF16).astype(F32)
    bscore = batch[:, 0:128]
    bcoef = LOSS_SCALE * jnp.exp(bscore - log_col)
    bweight = (bcoef * batch[:, 128:256]).astype(BF16).astype(F32)
    extras[:, 128:256] = bweight
    extras[:, 256:384] = bcoef * bscore
    extras_copy = pltpu.make_async_copy(extras, extras_out, extras_sem.at[0])
    extras_copy.start()
    onehot = listed_onehot(meta)
    spread_weight = jnp.where(onehot, value, 0.0)
    wb = spread_weight.astype(BF16)
    scalar = jnp.sum(jnp.where(onehot, coef * score, 0.0), axis=1, keepdims=True)

    rows = [jnp.sum(bcoef * bscore, axis=0, keepdims=True)]
    for s in range(4):
        rows.append(
            jnp.sum(bweight * batch[:, 256 + s * 128 : 384 + s * 128], axis=0, keepdims=True)
        )
    rows += [stats[i : i + 1, :] for i in range(13)]
    cols = stack_rows(rows, 128).T

    def col(i):
        return cols[:, i : i + 1]

    pinv = col(17)
    scale = (scalar + col(0)) * pinv * pinv
    g = gain[...]
    gp = dot(wb, qslot[:, 0:1024], ((1,), (0,)))
    bt = jnp.concatenate([bweight, jnp.zeros((96, 128), F32)], axis=0).T.astype(BF16)
    qpad = jnp.concatenate([qown[...], jnp.zeros((96, 1024), BF16)], axis=0)
    gp = gp + dot(bt, qpad, ((1,), (0,))) - scale * pooled[...].astype(F32)
    gg = gp * g
    leaving = [extras_copy]
    for s in range(4):
        arriving[s].wait()
        x = stream[s * 128 : s * 128 + 128, :]
        a, inv = col(5 + s), col(9 + s)
        inner = (
            jnp.sum(spread_weight * slot[2 + s : 3 + s, :], axis=1, keepdims=True)
            + col(1 + s)
            - scale * col(13 + s)
        )
        beta = inv * inv * a * inner / 4096.0
        ordered[s * 128 : s * 128 + 128, :] = (a * gg - beta * x).astype(BF16)
    token = iota((512, 512), 0)
    order = ((token & 3) * 128 + (token >> 2) == iota((512, 512), 1)).astype(F32).astype(BF16)
    grad[...] = dot(order, ordered[...], ((1,), (0,))).astype(BF16)
    leaving += [move(grad, grad_out, out_sems, s) for s in range(4)]
    lora[...] = dot(up[...], grad[...], ((1,), (1,)))
    up_part[...] = dot(middle[...], ordered[...], ((1,), (0,)))
    for k in range(4):
        fetch.wait(k)
        for i, out in enumerate((far_top, far_low)):
            out[:, k * 256 : k * 256 + 256] = dot(
                grad[i * 256 : i * 256 + 256, :], buffer[k * 256 : k * 256 + 256, :], ((1,), (1,))
            ).astype(BF16)
    for copy in leaving:
        copy.wait()


def sides_back_kernel(
    grad_in, weight,
    right_low, left_top, right_top, left_low,
    buffer, buffer2, sems, sems2, grad, in_sems,
):
    arriving = [move(grad_in, grad, in_sems, s) for s in range(4)]
    fetch = Fetch(weight, buffer, sems, 1)
    fetch2 = Fetch(weight, buffer2, sems2, 3)
    for copy in arriving:
        copy.wait()
    for fetched, low, top in ((fetch, right_low, right_top), (fetch2, left_low, left_top)):
        for k in range(4):
            fetched.wait(k)
            part = fetched.buffer[k * 256 : k * 256 + 256, :]
            columns = slice(k * 256, k * 256 + 256)
            top[:, columns] = dot(grad[0:256, :], part, ((1,), (1,))).astype(top.dtype)
            low[:, columns] = dot(grad[256:512, :], part, ((1,), (1,))).astype(low.dtype)


def join_kernel(l0, l1, l2, l3, tokens, up_part, adapter, lora_back):
    lora = (2.0 * ((l0[...] + l2[...]) + (l1[...] + l3[...]))).astype(BF16)
    lora_back[...] = lora
    adapter[0:16, :] = dot(lora, tokens[...], ((1,), (0,))).astype(BF16)
    adapter[16:32, :] = up_part[...].astype(BF16)


def add_kernel(right_top, left_low, via_right, via_left, to_right, to_left):
    to_right[...] = (right_top[...].astype(F32) + via_right[...].astype(F32)).astype(BF16)
    to_left[...] = (left_low[...].astype(F32) + via_left[...].astype(F32)).astype(BF16)


def pair_kernel(a, b, out):
    out[...] = (a[...].astype(F32) + b[...].astype(F32)).astype(BF16)


def four_sum(parts):
    a, b, c, d = [part[...].astype(F32) for part in parts]
    return (a + c) + (b + d)


def four_kernel(a, b, c, d, out):
    out[...] = four_sum((a, b, c, d)).astype(BF16)


def last_kernel(a, b, c, d, down, up):
    total = four_sum((a, b, c, d))
    down[...] = total[0:16]
    up[...] = 2.0 * total[16:32]


def finish_kernel(before, from_left, from_right, out):
    out[0:256, :] = (before[0:256, :] + from_left[...].astype(F32)).astype(BF16)
    out[256:512, :] = (before[256:512, :] + from_right[...].astype(F32)).astype(BF16)


def own_back_kernel(
    grad_in, weight, down, lora_back, from_right, from_left, out, buffer, sems, grad, in_sems
):
    arriving = [move(grad_in, grad, in_sems, s) for s in range(4)]
    fetch = Fetch(weight, buffer, sems, 0)
    local = dot(lora_back[...], down_rows(down, 0), ((0,), (0,)))
    for copy in arriving:
        copy.wait()
    for k in range(4):
        fetch.wait(k)
        lanes = slice(k * 256, k * 256 + 256)
        own = local[:, lanes] + dot(grad[...], buffer[k * 256 : k * 256 + 256, :], ((1,), (1,)))
        out[0:256, lanes] = own[0:256] + from_right[:, lanes].astype(F32)
        out[256:512, lanes] = own[256:512] + from_left[:, lanes].astype(F32)


def query_kernel(
    recv, home, extras, batch, pooled, qown, arrived, gradient, loss, listed
):
    group = lax.rem(lax.axis_index("dp"), 4) * 32
    place = iota((128, 1024), 0) == (iota((128, 1024), 1) & 31) + group
    place = place.astype(F32).astype(BF16)
    spread = iota((32, 1024), 0) == (iota((32, 1024), 1) >> 5)
    sub = iota((32, 128), 0)

    def by_slot(lanes):
        table = jnp.zeros((32, 128), F32)
        for d in range(32):
            table = jnp.where(sub == d, recv[d, :, lanes], table)
        wide = jnp.zeros((32, 1024), F32)
        for part in split3(table):
            wide += dot(part.astype(BF16), place, ((1,), (0,)))
        return jnp.sum(jnp.where(spread, wide, 0.0), axis=0, keepdims=True)

    score, pre = by_slot(slice(1024, 1152)), by_slot(slice(1152, 1280))
    mine, first, used = home[0:32, :], home[33:34, :], home[34:35, :] > 0.0
    log_col = extras[:, 0:1]
    log_slot = jnp.sum(mine * log_col, axis=0, keepdims=True)
    coef = jnp.where(used, LOSS_SCALE * (jnp.exp(score - log_slot) - first), 0.0)
    value = jnp.where(used, coef * pre, 0.0).astype(BF16).astype(F32)
    score = jnp.where(used, score, 0.0)
    positive = jnp.sum(mine * (first * score), axis=1, keepdims=True)
    scalar = jnp.sum(mine * (coef * score), axis=1, keepdims=True)
    scalar = scalar + jnp.sum(extras[:, 256:384], axis=1, keepdims=True)
    eye = iota((32, 128), 0) == iota((32, 128), 1)
    row = jnp.sum(jnp.where(eye, log_col - positive, 0.0), axis=0, keepdims=True)
    loss[...] = row[:, 0:32]
    qinv = batch[:, 768:769]
    last = last_rows(arrived[:, 1024:1152], 1024)
    for c in range(4):
        rows = unfold(arrived[c * 192 : c * 192 + 192, 0:1024].astype(F32), last, c * 8)
        listed[c * 256 : c * 256 + 256, :] = rows.astype(BF16)
    total = dot((mine * value).astype(BF16), listed[...], ((1,), (0,)))
    total = total + dot(extras[:, 128:256].astype(BF16), pooled[...], ((1,), (0,)))
    gradient[...] = (total - (scalar * qinv * qinv) * qown[...].astype(F32)).astype(BF16)


ANY, HOLD, LOAD, STORE = "any", "hold", "load", "store"


def call(kernel, outs, args, scratch=(), limit=16, cost=None):
    in_specs, values, moved = [], [], []
    for place, arg in enumerate(args):
        space = pltpu.VMEM
        if isinstance(arg, tuple):
            arg, mark = arg
            space = pltpu.HBM
            if mark != ANY:
                arg = pltpu.with_memory_space_constraint(arg, pltpu.HBM)
            if mark == LOAD:
                moved.append((place, arg.shape, arg.dtype))
        values.append(arg)
        in_specs.append(pl.BlockSpec(memory_space=space))
    loads = len(moved)
    for place, (shape, dtype, *mark) in enumerate(outs):
        if mark == [STORE]:
            moved.append((len(args) + place, shape, dtype))
    count, extra = len(args) + len(outs), len(moved)

    def whole(*refs):
        refs = list(refs)
        if not extra:
            return kernel(*refs)
        sems = refs.pop()
        buffers = [refs.pop() for _ in range(extra)][::-1]
        copies = []
        for i, (place, _, _) in enumerate(moved):
            ends = (refs[place], buffers[i]) if i < loads else (buffers[i], refs[place])
            copies.append(pltpu.make_async_copy(*ends, sems.at[i]))
            refs[place] = buffers[i]
        for copy in copies[:loads]:
            copy.start()
        for copy in copies[:loads]:
            copy.wait()
        kernel(*refs)
        for copy in copies[loads:]:
            copy.start()
        for copy in copies[loads:]:
            copy.wait()

    scratch = list(scratch)
    if extra:
        scratch += [pltpu.VMEM(shape, dtype) for _, shape, dtype in moved]
        scratch.append(pltpu.SemaphoreType.DMA((extra,)))
    if cost is not None:
        cost = pl.CostEstimate(flops=int(cost * 1.15e9), bytes_accessed=0, transcendentals=0)
    return pl.pallas_call(
        whole,
        cost_estimate=cost,
        name=kernel.__name__,
        out_shape=[
            (pltpu.HBM if mark else jax.ShapeDtypeStruct)(s, t) for s, t, *mark in outs
        ],
        in_specs=in_specs,
        out_specs=[
            pl.BlockSpec(memory_space=pltpu.HBM if mark else pltpu.VMEM) for _, _, *mark in outs
        ],
        scratch_shapes=scratch,
        compiler_params=pltpu.CompilerParams(vmem_limit_bytes=limit * 2**20),
    )(*values)


COST_OWN = 15.0
COST_PAIR = 3.0
COST_JOIN = 16.0
COST_GRAD = 1.0
COST_FAR = 4.0
COST_SIDES = 1.0
WEIGHT_BUFFER = pltpu.VMEM((1024, 1024), BF16)
FOUR = pltpu.SemaphoreType.DMA((4,))


def ring(x, step):
    return lax.ppermute(x, "mp", [(i, (i + step) % 4) for i in range(4)])


def ring_sum(x):
    return (x + ring(x, 2)) + (ring(x, 1) + ring(x, 3))


def grid_index(x, y, core):
    return (x * 4 + y) * 2 + core


def grid_shift(v, axis, step):
    pairs = []
    for x in range(4):
        for y in range(4):
            for core in range(2):
                if axis == "core":
                    to = (x, y, 1 - core)
                elif axis == "x":
                    to = ((x + step) % 4, y, core)
                else:
                    to = (x, (y + step) % 4, core)
                pairs.append((grid_index(x, y, core), grid_index(*to)))
    return lax.ppermute(v, "dp", pairs)


def grid_sum(x, own, query):
    shape = x.shape
    tie = lax.optimization_barrier
    (x,) = call(pair_kernel, [(shape, BF16)], [x, grid_shift(x, "core", 1)], cost=COST_PAIR)
    parts = [x] + [grid_shift(x, "x", step) for step in (1, 2, 3)]
    own, *parts = tie((own, *parts))
    (x,) = call(four_kernel, [(shape, BF16)], parts)
    parts = [x] + [grid_shift(x, "y", step) for step in (1, 2, 3)]
    query, own, *parts = tie((query, own, *parts))
    down, up = call(last_kernel, [((16, 1024), F32), ((16, 1024), F32)], parts)
    return down, up, own, query


def body(
    attention_output,
    residual,
    output_projection_weight,
    adapter_down_matrix,
    adapter_up_matrix,
    final_norm_gain,
    query_hidden_states,
    pair_passage_index,
    lengths,
):
    weight = (output_projection_weight, HOLD)
    down = adapter_down_matrix.T
    up = adapter_up_matrix
    qown = query_hidden_states
    half, full = (256, 1024), (512, 1024)
    tie = lax.optimization_barrier

    top, low = call(
        order_kernel, [(half, BF16), (half, BF16)], [(attention_output, LOAD)]
    )
    with jax.named_scope("leg1"):
        left_top, right_low = ring(top, 1), ring(low, 3)

    ids, _, _ = tie((pair_passage_index, top, low))
    flat = jnp.pad(ids.reshape(-1), (0, 640 - 544), constant_values=-1)
    qslot_out, home = call(
        slot_kernel,
        [((768, 1280), BF16, STORE), ((40, 1024), F32, STORE)],
        [flat.reshape(1, 640), flat.reshape(640, 1), qown],
    )
    with jax.named_scope("a2a_queries"):
        qslot = lax.all_to_all(qslot_out, "dp", 0, 0, tiled=True)
    with jax.named_scope("leg2"):
        left_low, right_top = ring(low, 1), ring(top, 3)
    with jax.named_scope("leg3"):
        far_top, far_low = ring(left_top, 1), ring(right_low, 3)

    residual_tied, left_top, right_low = tie((residual, left_top, right_low))
    stream, middle = call(
        own_kernel,
        [(full, F32), ((16, 512), F32)],
        [top, low, residual_tied, weight, down],
        [WEIGHT_BUFFER, FOUR], limit=24, cost=COST_OWN,
    )
    stream, middle = call(
        sides_kernel,
        [(full, F32, STORE), ((16, 512), F32)],
        [left_top, left_low, right_top, right_low, stream, middle, weight, down],
        [WEIGHT_BUFFER, WEIGHT_BUFFER, FOUR, FOUR], limit=24,
    )
    gain = final_norm_gain.astype(F32).reshape(1, 1024)
    stream, middle, tokens, table = call(
        far_kernel,
        [(full, F32, ANY), ((16, 512), BF16), (full, BF16), ((16, 128), F32)],
        [far_top, far_low, (stream, HOLD), middle, weight, down, up, gain],
        [WEIGHT_BUFFER, FOUR, pltpu.VMEM(full, F32), FOUR, pltpu.VMEM(full, F32), FOUR],
        limit=24,
        cost=COST_FAR,
    )
    qslot, table = tie((qslot, table))
    qslot, meta, turned = call(
        meta_kernel,
        [((1024, 1152), BF16), ((40, 1024), F32), ((1024, 1024), BF16)],
        [(qslot, HOLD)],
        [
            pltpu.VMEM((768, 1152), BF16), pltpu.VMEM((768, 128), BF16),
            pltpu.SemaphoreType.DMA((5,)),
        ],
    )
    (pack,) = call(partial_kernel, [((24, 1024), F32)], [tokens, turned, qown, meta, table])
    with jax.named_scope("packs"):
        packs = [pack, ring(pack, 1), ring(pack, 2), ring(pack, 3)]
    slot, batch, stats, sums = call(
        score_kernel,
        [((8, 1024), F32), ((32, 896), F32), ((16, 128), F32), ((32, 1, 1280), F32)],
        [*packs, meta, lengths.reshape(1, 128)],
    )
    with jax.named_scope("a2a_sums"):
        recv = lax.all_to_all(sums, "dp", 0, 0, tiled=True)
    pooled, rows = call(
        pooled_kernel,
        [((128, 1024), BF16), ((768, 1152), BF16)],
        [(stream, HOLD), stats, gain, qslot],
        [pltpu.VMEM(full, F32), FOUR],
    )
    grad, far_top, far_low, lora, extras, up_part = call(
        gradient_kernel,
        [
            (full, BF16, ANY), (half, BF16), (half, BF16), ((16, 512), F32),
            ((32, 384), F32, ANY), ((16, 1024), F32),
        ],
        [recv, (stream, HOLD), qslot, qown, gain, meta, slot, batch, stats, pooled, up, middle, weight],
        [
            WEIGHT_BUFFER, FOUR, pltpu.VMEM(full, F32), FOUR, pltpu.VMEM(full, BF16), FOUR,
            pltpu.VMEM((32, 384), F32), pltpu.SemaphoreType.DMA((1,)), pltpu.VMEM(full, BF16),
        ],
        limit=24, cost=COST_GRAD,
    )

    far_top, far_low, rows = tie((far_top, far_low, rows))
    with jax.named_scope("back1"):
        via_right, via_left = ring(far_top, 1), ring(far_low, 3)
    with jax.named_scope("lora_sum"):
        loras = [lora, ring(lora, 1), ring(lora, 2), ring(lora, 3)]
    with jax.named_scope("a2a_rows"):
        arrived = lax.all_to_all(rows, "dp", 0, 0, tiled=True)
    right_low, left_top, right_top, left_low = call(
        sides_back_kernel,
        [(half, BF16), (half, BF16), (half, BF16), (half, BF16)],
        [(grad, ANY), weight],
        [WEIGHT_BUFFER, WEIGHT_BUFFER, FOUR, FOUR, pltpu.VMEM(full, BF16), FOUR],
        limit=24,
        cost=COST_SIDES,
    )
    with jax.named_scope("back2"):
        to_right_low, to_left_top = ring(right_low, 1), ring(left_top, 3)
    right_top, left_low = call(
        add_kernel,
        [(half, BF16), (half, BF16)],
        [right_top, left_low, via_right, via_left],
    )
    right_top, left_low, up_part = tie((right_top, left_low, up_part))
    adapter, lora_back = call(
        join_kernel,
        [((32, 1024), BF16), ((16, 512), BF16)],
        [*loras, (attention_output, LOAD), up_part],
        cost=COST_JOIN,
    )
    with jax.named_scope("back3"):
        to_right_top, to_left_low = ring(right_top, 1), ring(left_low, 3)
    (before,) = call(
        own_back_kernel,
        [(full, F32)],
        [(grad, ANY), weight, down, lora_back, to_left_top, to_right_low],
        [WEIGHT_BUFFER, FOUR, pltpu.VMEM(full, BF16), FOUR],
        limit=24,
    )
    query_gradient, loss = call(
        query_kernel,
        [((32, 1024), BF16), ((1, 32), F32)],
        [
            (recv, LOAD), (home, LOAD), (extras, LOAD), (batch, LOAD), (pooled, LOAD),
            (qown, LOAD), arrived,
        ],
        [pltpu.VMEM((1024, 1024), BF16)],
    )
    with jax.named_scope("adapters"):
        down_grad, up_grad, before, query_gradient = grid_sum(adapter, before, query_gradient)
    (attention_gradient,) = call(
        finish_kernel,
        [(full, BF16)],
        [before, to_right_top, to_left_low],
    )
    return (
        loss.reshape(32),
        query_gradient,
        grad,
        attention_gradient,
        down_grad.T,
        up_grad,
    )


def solution(mesh):
    in_specs = (
        P("dp", "mp"),
        P("dp", "mp"),
        P(None, "mp"),
        P(),
        P(None, "mp"),
        P("mp"),
        P("dp", "mp"),
        P("dp", None),
        P("dp"),
    )
    out_specs = (P("dp"), P("dp", "mp"), P("dp", "mp"), P("dp", "mp"), P("mp", None), P(None, "mp"))
    return jax.shard_map(body, mesh=mesh, in_specs=in_specs, out_specs=out_specs, check_vma=False)
```

```python
import jax
import jax.numpy as jnp
from jax import lax
from jax.experimental import pallas as pl
from jax.experimental.pallas import tpu as pltpu
from jax.sharding import PartitionSpec as P

F32 = jnp.float32
BF16 = jnp.bfloat16
INV_TEMPER = 1.0 / 0.02
LOSS_SCALE = 1024.0
SLOTS = 32
HARD = 17
PAIRS = [(a, b) for a in range(4) for b in range(a, 4)]


def dot(a, b, dims):
    return lax.dot_general(a, b, ((dims[0], dims[1]), ((), ())), preferred_element_type=F32)


def split3(x):
    a = x.astype(BF16).astype(F32)
    b = (x - a).astype(BF16).astype(F32)
    return [a, b, x - a - b]


def iota(shape, dim):
    return lax.broadcasted_iota(jnp.int32, shape, dim)


def stack_rows(rows, height):
    where = iota((height, rows[0].shape[1]), 0)
    total = jnp.zeros((height, rows[0].shape[1]), F32)
    for place, row in enumerate(rows):
        total = jnp.where(where == place, row, total)
    return total


def step_of(offset):
    return lax.rem(lax.axis_index("mp") + offset, 4)


class Fetch:
    def __init__(self, weight, buffer, sems, offset):
        base = step_of(offset) * 1024
        self.buffer = buffer
        self.copies = [
            pltpu.make_async_copy(
                weight.at[pl.ds(pl.multiple_of(base + k * 256, 256), 256), :],
                buffer.at[pl.ds(k * 256, 256), :],
                sems.at[k],
            )
            for k in range(4)
        ]
        for copy in self.copies:
            copy.start()

    def wait(self, k):
        self.copies[k].wait()


def move(source, target, sems, part):
    rows = pl.ds(part * 128, 128)
    copy = pltpu.make_async_copy(source.at[rows, :], target.at[rows, :], sems.at[part])
    copy.start()
    return copy


def down_rows(down, offset):
    return down[:, pl.ds(pl.multiple_of(step_of(offset) * 1024, 1024), 1024)]


def forward_dot(blocks, fetch, first):
    out = list(first)
    for k in range(4):
        fetch.wait(k)
        part = fetch.buffer[k * 256 : k * 256 + 256, :]
        for i, block in enumerate(blocks):
            out[i] = out[i] + dot(block[:, k * 256 : k * 256 + 256], part, ((1,), (0,)))
    return out


def order_kernel(tokens, top, low):
    for i, out in enumerate((top, low)):
        row = iota((256, 512), 0) + i * 256
        order = ((row & 127) * 4 + (row >> 7) == iota((256, 512), 1)).astype(F32).astype(BF16)
        out[...] = dot(order, tokens[...], ((1,), (0,))).astype(BF16)


def fold_map(shape, slot_dim):
    part = iota(shape, 1 - slot_dim)
    return iota(shape, slot_dim) == (part & 31) * 24 + (part >> 5)


def fold(pieces, last, out):
    width = last.shape[1]
    off = 0
    for piece in pieces:
        lanes = slice(off, off + piece.shape[1])
        kept = [piece[o * 32 : o * 32 + 24] for o in range(32)]
        out[:, lanes] = jnp.concatenate(kept, axis=0).astype(BF16)
        off += piece.shape[1]
    stack = jnp.concatenate([last[:, i : i + 128] for i in range(0, width, 128)], axis=0)
    table = fold_map((768, stack.shape[0]), 0).astype(F32).astype(BF16)
    out[:, width : width + 128] = dot(table, stack, ((1,), (0,))).astype(BF16)


def last_rows(extra, width):
    parts = width // 128
    table = fold_map((parts * 32, 768), 1).astype(F32).astype(BF16)
    stack = dot(table, extra, ((1,), (0,)))
    last = jnp.concatenate([stack[c * 32 : c * 32 + 32] for c in range(parts)], axis=1)
    last = jnp.concatenate([last, jnp.zeros((96, width), F32)], axis=0).astype(BF16)
    place = (iota((256, 128), 0) == iota((256, 128), 1) * 8).astype(F32).astype(BF16)
    return dot(place, last, ((1,), (0,)))


def unfold(kept, last, first):
    pieces = []
    for i in range(8):
        pieces.append(kept[i * 24 : i * 24 + 24])
        pieces.append(last[(first + i) * 8 : (first + i) * 8 + 8])
    return jnp.concatenate(pieces, axis=0)


def last_slots():
    return (iota((32, 1024), 1) == iota((32, 1024), 0) * 32 + 24).astype(F32).astype(BF16)


def slot_kernel(ids_row, ids_col, queries, out, home):
    ids = ids_row[...]
    owner = iota((32, 640), 0)
    owned = (ids >> 7) == owner
    before = (iota((640, 640), 0) < iota((640, 640), 1)).astype(F32).astype(BF16)
    rank = dot(owned.astype(F32).astype(BF16), before, ((1,), (0,)))
    slot = jnp.sum(jnp.where(owned, rank + (owner * SLOTS).astype(F32), 0.0), axis=0, keepdims=True)
    slot = jnp.where(ids < 0, -1.0, slot).astype(jnp.int32)
    listed = (iota((1024, 640), 0) == slot).astype(F32).astype(BF16)
    entry, lane = iota((640, 128), 0), iota((640, 128), 1)
    query = (entry * 241) >> 12
    values = jnp.where(lane < 32, (query == lane).astype(F32), 0.0)
    values = jnp.where(lane == 32, (ids_col[...] & 127).astype(F32), values)
    values = jnp.where((lane == 33) & (query * HARD == entry), 1.0, values)
    values = jnp.where(lane == 34, 1.0, values)
    picked = dot(listed, values.astype(BF16), ((1,), (0,)))
    q = queries[...].astype(F32)
    squares = jnp.sum(q * q, axis=1, keepdims=True)
    square_row = jnp.sum(
        jnp.where(iota((32, 128), 0) == iota((32, 128), 1), squares, 0.0), axis=0, keepdims=True
    )
    lane = iota((1024, 128), 1)
    mine = jnp.where(lane < 32, picked, 0.0)
    square = jnp.sum(mine * square_row, axis=1, keepdims=True)
    for i, part in enumerate(split3(square)):
        picked = jnp.where(lane == 35 + i, part, picked)
    home[...] = picked.T[0:40, :]
    padded = jnp.concatenate([queries[...], jnp.zeros((96, 1024), BF16)], axis=0)
    rows = dot(mine.astype(BF16), padded, ((1,), (0,)))
    last = dot(last_slots(), mine.astype(BF16), ((1,), (0,))).astype(BF16)
    last = dot(last, padded, ((1,), (0,))).astype(BF16)
    last_values = dot(last_slots(), picked.astype(BF16), ((1,), (0,))).astype(BF16)
    fold([rows, picked], jnp.concatenate([last, last_values], axis=1), out)


def meta_kernel(arrived, qslot, meta, turned, main, extra, sems):
    copies = [pltpu.make_async_copy(arrived.at[:, 1152:1280], extra, sems.at[4])]
    for c in range(4):
        rows = pl.ds(c * 192, 192)
        copies.append(pltpu.make_async_copy(arrived.at[rows, 0:1152], main.at[rows, :], sems.at[c]))
    for copy in copies:
        copy.start()
    copies[0].wait()
    last = last_rows(extra[...], 1152)
    for c in range(4):
        copies[c + 1].wait()
        rows = unfold(main[c * 192 : c * 192 + 192, :].astype(F32), last, c * 8)
        lanes = slice(c * 256, c * 256 + 256)
        qslot[lanes, :] = rows.astype(BF16)
        turned[:, lanes] = rows[:, 0:1024].T.astype(BF16)
        meta[0:40, lanes] = rows[:, 1024:1152].T[0:40]
    meta[35:36, :] = meta[35:36, :] + meta[36:37, :] + meta[37:38, :]


def own_kernel(top, low, residual, weight, down, stream, middle, buffer, sems):
    fetch = Fetch(weight, buffer, sems, 0)
    first = []
    for i in range(2):
        row = iota((256, 512), 0) + i * 256
        order = ((row & 127) * 4 + (row >> 7) == iota((256, 512), 1)).astype(F32).astype(BF16)
        first.append(dot(order, residual[...], ((1,), (0,))))
    d = down_rows(down, 0)
    middle[:, 0:256] = dot(d, top[...], ((1,), (1,)))
    middle[:, 256:512] = dot(d, low[...], ((1,), (1,)))
    out = forward_dot([top, low], fetch, first)
    stream[0:256, :] = out[0]
    stream[256:512, :] = out[1]


def sides_kernel(
    left_top, left_low, right_top, right_low, before, middle_before, weight, down,
    stream, middle, buffer, buffer2, sems, sems2,
):
    fetch = Fetch(weight, buffer, sems, 3)
    fetch2 = Fetch(weight, buffer2, sems2, 1)
    d, d2 = down_rows(down, 3), down_rows(down, 1)
    middle[:, 0:256] = (
        middle_before[:, 0:256]
        + dot(d, left_top[...], ((1,), (1,)))
        + dot(d2, right_top[...], ((1,), (1,)))
    )
    middle[:, 256:512] = (
        middle_before[:, 256:512]
        + dot(d, left_low[...], ((1,), (1,)))
        + dot(d2, right_low[...], ((1,), (1,)))
    )
    out = forward_dot([left_top, left_low], fetch, [before[0:256, :], before[256:512, :]])
    out = forward_dot([right_top, right_low], fetch2, out)
    stream[0:256, :] = out[0]
    stream[256:512, :] = out[1]


def listed_onehot(meta):
    return (iota((128, 1024), 0).astype(F32) == meta[32:33, :]) & (meta[34:35, :] > 0.0)


def far_kernel(
    far_top, far_low, before_in, middle_before, weight, down, up, gain,
    stream_out, middle, tokens, table_out, buffer, sems, stream, out_sems, before, in_sems,
):
    fetch = Fetch(weight, buffer, sems, 2)
    arriving = [move(before_in, before, in_sems, s) for s in range(4)]
    d = down_rows(down, 2)
    mid = [
        (middle_before[:, i * 256 : i * 256 + 256] + dot(d, far[...], ((1,), (1,)))).astype(BF16)
        for i, far in enumerate((far_top, far_low))
    ]
    out = [2.0 * dot(mid[i], up[...], ((0,), (0,))) for i in range(2)]
    middle[:, 0:256] = mid[0]
    middle[:, 256:512] = mid[1]
    out = forward_dot([far_top, far_low], fetch, out)
    g = gain[...]
    columns = []
    scaled = []
    sent = []
    for s in range(4):
        arriving[s].wait()
        x = out[s // 2][(s % 2) * 128 : (s % 2) * 128 + 128] + before[s * 128 : s * 128 + 128, :]
        stream[s * 128 : s * 128 + 128, :] = x
        sent.append(move(stream, stream_out, out_sems, s))
        u = x * g
        scaled.append(u)
        columns.append(jnp.sum(x * x, axis=1, keepdims=True))
        tokens[s * 128 : s * 128 + 128, :] = u.astype(BF16)
    for a, b in PAIRS:
        columns.append(jnp.sum(scaled[a] * scaled[b], axis=1, keepdims=True))
    lane = iota((128, 128), 1)
    table = jnp.zeros((128, 128), F32)
    for place, column in enumerate(columns):
        table = jnp.where(lane == place, column, table)
    table_out[...] = table.T[0:16]
    for copy in sent:
        copy.wait()


def partial_kernel(tokens, turned, qown, meta, table, pack):
    onehot = listed_onehot(meta)
    batch = dot(qown[...], tokens[...], ((1,), (1,)))
    pack[0:16, 0:512] = batch[0:16]
    pack[0:16, 512:1024] = batch[16:32]
    for j in range(4):
        lanes = slice(j * 256, j * 256 + 256)
        scores = dot(tokens[...], turned[:, lanes], ((1,), (0,)))
        for s in range(4):
            pack[16 + s : 17 + s, lanes] = jnp.sum(
                jnp.where(onehot[:, lanes], scores[s * 128 : s * 128 + 128], 0.0),
                axis=0,
                keepdims=True,
            )
    pack[20:21, :] = meta[35:36, :]
    pack[21:23, :] = jnp.zeros((2, 1024), F32)
    for place in range(4 + len(PAIRS)):
        row, off = 21 + place // 8, (place % 8) * 128
        pack[row : row + 1, off : off + 128] = table[place : place + 1, :]
    q = qown[...].astype(F32)
    squares = jnp.sum(q * q, axis=1, keepdims=True)
    pack[23:24, 0:128] = jnp.sum(
        jnp.where(iota((32, 128), 0) == iota((32, 128), 1), squares, 0.0), axis=0, keepdims=True
    )
    pack[23:24, 128:1024] = jnp.zeros((1, 896), F32)


def score_kernel(p0, p1, p2, p3, meta, lens, slot, batch, stats, sums):
    def total(rows, lanes):
        return (p0[rows, lanes] + p2[rows, lanes]) + (p1[rows, lanes] + p3[rows, lanes])

    def stat(place):
        row, off = 21 + place // 8, (place % 8) * 128
        return total(slice(row, row + 1), slice(off, off + 128))

    every = slice(0, 1024)
    used = meta[34:35, :] > 0.0
    length = lens[...].astype(F32)
    inv = [lax.rsqrt(stat(s) / 4096.0 + 1e-05) for s in range(4)]
    a = [jnp.where(s < length, inv[s] / length, 0.0) for s in range(4)]
    gram = {pair: stat(4 + i) for i, pair in enumerate(PAIRS)}
    toward = [
        sum(a[t] * gram[(min(s, t), max(s, t))] for t in range(4)) for s in range(4)
    ]
    square = sum(a[s] * toward[s] for s in range(4))
    pinv = lax.rsqrt(square + 1e-06)
    rows = []
    for row in a + [pinv]:
        rows += split3(row)
    onehot = jnp.where(listed_onehot(meta), 1.0, 0.0).astype(BF16)
    picked = dot(stack_rows(rows, 16).astype(BF16), onehot, ((1,), (0,)))
    pick = [
        picked[3 * i : 3 * i + 1] + picked[3 * i + 1 : 3 * i + 2] + picked[3 * i + 2 : 3 * i + 3]
        for i in range(5)
    ]
    dots = [total(slice(16 + s, 17 + s), every) for s in range(4)]
    product = pick[0] * dots[0] + pick[1] * dots[1] + pick[2] * dots[2] + pick[3] * dots[3]
    qinv = lax.rsqrt(total(slice(20, 21), every) + 1e-06)
    pre = qinv * pick[4] * INV_TEMPER
    score = product * pre
    grown = jnp.where(used, jnp.exp(score), 0.0)
    slot[0:1, :] = score
    slot[1:2, :] = pre
    for s in range(4):
        slot[2 + s : 3 + s, :] = dots[s]
    slot[6:8, :] = jnp.zeros((2, 1024), F32)

    own = total(slice(23, 24), slice(0, 128))
    lane = iota((32, 128), 1)
    qcol = lax.rsqrt(
        jnp.sum(jnp.where(lane == iota((32, 128), 0), own, 0.0), axis=1, keepdims=True) + 1e-06
    )
    pieces = []
    for s in range(4):
        top = total(slice(0, 16), slice(s * 128, s * 128 + 128))
        low = total(slice(0, 16), slice(512 + s * 128, 640 + s * 128))
        pieces.append(jnp.concatenate([top, low], axis=0))
        batch[:, 256 + s * 128 : 384 + s * 128] = pieces[s]
    bpre = qcol * pinv * INV_TEMPER
    bscore = sum(a[s] * pieces[s] for s in range(4)) * bpre
    bgrown = jnp.exp(bscore)
    batch[:, 0:128] = bscore
    batch[:, 128:256] = bpre
    batch[:, 768:896] = jnp.broadcast_to(qcol, (32, 128))

    stats[...] = stack_rows(a + inv + toward + [pinv], 16)

    mine = meta[0:32, :]
    block = ((iota((1024, 128), 0) >> 5) == iota((1024, 128), 1)).astype(F32).astype(BF16)

    def by_query(row):
        out = jnp.zeros((32, 128), F32)
        for part in split3(row):
            out += dot((mine * part).astype(BF16), block, ((1,), (0,)))
        return out

    at_home = lane == lax.axis_index("dp")
    exp_sum = by_query(grown) + jnp.where(at_home, jnp.sum(bgrown, axis=1, keepdims=True), 0.0)
    place = ((iota((128, 1024), 1) & 31) == iota((128, 1024), 0)).astype(F32).astype(BF16)
    wide = jnp.zeros((32, 1024), F32)
    for part in split3(exp_sum):
        wide += dot(part.astype(BF16), place, ((1,), (0,)))
    spread = iota((32, 1024), 0) == (iota((32, 1024), 1) >> 5)
    exp_row = jnp.sum(jnp.where(spread, wide, 0.0), axis=0, keepdims=True)
    for b in range(32):
        group = slice(b // 4 * 128, b // 4 * 128 + 128)
        sums[b, :, 0:1024] = exp_row
        sums[b, :, 1024:1152] = score[:, group]
        sums[b, :, 1152:1280] = pre[:, group]


def pooled_kernel(stream_in, stats, gain, qslot, pooled, rows, stream, sems):
    for copy in [move(stream_in, stream, sems, s) for s in range(4)]:
        copy.wait()
    cols = jnp.concatenate([stats[...], jnp.zeros((112, 128), F32)], axis=0).T
    g = gain[...]
    mean = sum(cols[:, s : s + 1] * (stream[s * 128 : s * 128 + 128, :] * g) for s in range(4))
    pooled[...] = mean.astype(BF16)
    meta = qslot[:, 1024:1152].astype(F32)
    lane = iota((1024, 128), 1).astype(F32)
    listed = ((meta[:, 32:33] == lane) & (meta[:, 34:35] > 0.0)).astype(F32).astype(BF16)
    full = dot(listed, pooled[...], ((1,), (0,)))
    last = dot(last_slots(), listed, ((1,), (0,))).astype(BF16)
    fold([full], dot(last, pooled[...], ((1,), (0,))).astype(BF16), rows)


def gradient_kernel(
    recv, stream_in, qslot, qown, gain, meta, slot, batch, stats, pooled, up, middle, weight,
    grad_out, far_top, far_low, lora, extras_out, up_part,
    buffer, sems, stream, in_sems, grad, out_sems, extras, extras_sem, ordered,
):
    arriving = [move(stream_in, stream, in_sems, s) for s in range(4)]
    fetch = Fetch(weight, buffer, sems, 2)
    total = recv[0, :, 0:1024]
    for b in range(1, 32):
        total = total + recv[b, :, 0:1024]
    log_row = jnp.log(total)
    spread = iota((32, 1024), 0) == (iota((32, 1024), 1) >> 5)
    place = ((iota((1024, 128), 0) & 31) == iota((1024, 128), 1)).astype(F32).astype(BF16)
    table = jnp.zeros((32, 128), F32)
    for part in split3(log_row):
        table += dot(jnp.where(spread, part, 0.0).astype(BF16), place, ((1,), (0,)))
    block = (iota((128, 1024), 0) == (iota((128, 1024), 1) >> 5)).astype(F32).astype(BF16)
    wide = jnp.zeros((32, 1024), F32)
    for part in split3(table):
        wide += dot(part.astype(BF16), block, ((1,), (0,)))
    log_slot = jnp.sum(meta[0:32, :] * wide, axis=0, keepdims=True)
    lane = iota((32, 128), 1)
    log_col = jnp.sum(
        jnp.where(lane == lax.axis_index("dp"), table, 0.0), axis=1, keepdims=True
    )
    extras[:, 0:128] = jnp.broadcast_to(log_col, (32, 128))
    used, first = meta[34:35, :] > 0.0, meta[33:34, :]
    score = slot[0:1, :]
    coef = jnp.where(used, LOSS_SCALE * (jnp.exp(score - log_slot) - first), 0.0)
    value = (coef * slot[1:2, :]).astype(BF16).astype(F32)
    bscore = batch[:, 0:128]
    bcoef = LOSS_SCALE * jnp.exp(bscore - log_col)
    bweight = (bcoef * batch[:, 128:256]).astype(BF16).astype(F32)
    extras[:, 128:256] = bweight
    extras[:, 256:384] = bcoef * bscore
    extras_copy = pltpu.make_async_copy(extras, extras_out, extras_sem.at[0])
    extras_copy.start()
    onehot = listed_onehot(meta)
    spread_weight = jnp.where(onehot, value, 0.0)
    wb = spread_weight.astype(BF16)
    scalar = jnp.sum(jnp.where(onehot, coef * score, 0.0), axis=1, keepdims=True)

    rows = [jnp.sum(bcoef * bscore, axis=0, keepdims=True)]
    for s in range(4):
        rows.append(
            jnp.sum(bweight * batch[:, 256 + s * 128 : 384 + s * 128], axis=0, keepdims=True)
        )
    rows += [stats[i : i + 1, :] for i in range(13)]
    cols = stack_rows(rows, 128).T

    def col(i):
        return cols[:, i : i + 1]

    pinv = col(17)
    scale = (scalar + col(0)) * pinv * pinv
    g = gain[...]
    gp = dot(wb, qslot[:, 0:1024], ((1,), (0,)))
    bt = jnp.concatenate([bweight, jnp.zeros((96, 128), F32)], axis=0).T.astype(BF16)
    qpad = jnp.concatenate([qown[...], jnp.zeros((96, 1024), BF16)], axis=0)
    gp = gp + dot(bt, qpad, ((1,), (0,))) - scale * pooled[...].astype(F32)
    gg = gp * g
    leaving = [extras_copy]
    for s in range(4):
        arriving[s].wait()
        x = stream[s * 128 : s * 128 + 128, :]
        a, inv = col(5 + s), col(9 + s)
        inner = (
            jnp.sum(spread_weight * slot[2 + s : 3 + s, :], axis=1, keepdims=True)
            + col(1 + s)
            - scale * col(13 + s)
        )
        beta = inv * inv * a * inner / 4096.0
        ordered[s * 128 : s * 128 + 128, :] = (a * gg - beta * x).astype(BF16)
    token = iota((512, 512), 0)
    order = ((token & 3) * 128 + (token >> 2) == iota((512, 512), 1)).astype(F32).astype(BF16)
    grad[...] = dot(order, ordered[...], ((1,), (0,))).astype(BF16)
    leaving += [move(grad, grad_out, out_sems, s) for s in range(4)]
    lora[...] = dot(up[...], grad[...], ((1,), (1,)))
    up_part[...] = dot(middle[...], ordered[...], ((1,), (0,)))
    for k in range(4):
        fetch.wait(k)
        for i, out in enumerate((far_top, far_low)):
            out[:, k * 256 : k * 256 + 256] = dot(
                grad[i * 256 : i * 256 + 256, :], buffer[k * 256 : k * 256 + 256, :], ((1,), (1,))
            ).astype(BF16)
    for copy in leaving:
        copy.wait()


def sides_back_kernel(
    grad_in, weight,
    right_low, left_top, right_top, left_low,
    buffer, buffer2, sems, sems2, grad, in_sems,
):
    arriving = [move(grad_in, grad, in_sems, s) for s in range(4)]
    fetch = Fetch(weight, buffer, sems, 1)
    fetch2 = Fetch(weight, buffer2, sems2, 3)
    for copy in arriving:
        copy.wait()
    for fetched, low, top in ((fetch, right_low, right_top), (fetch2, left_low, left_top)):
        for k in range(4):
            fetched.wait(k)
            part = fetched.buffer[k * 256 : k * 256 + 256, :]
            columns = slice(k * 256, k * 256 + 256)
            top[:, columns] = dot(grad[0:256, :], part, ((1,), (1,))).astype(top.dtype)
            low[:, columns] = dot(grad[256:512, :], part, ((1,), (1,))).astype(low.dtype)


def join_kernel(l0, l1, l2, l3, tokens, up_part, adapter, lora_back):
    lora = (2.0 * ((l0[...] + l2[...]) + (l1[...] + l3[...]))).astype(BF16)
    lora_back[...] = lora
    adapter[0:16, :] = dot(lora, tokens[...], ((1,), (0,))).astype(BF16)
    adapter[16:32, :] = up_part[...].astype(BF16)


def add_kernel(right_top, left_low, via_right, via_left, to_right, to_left):
    to_right[...] = (right_top[...].astype(F32) + via_right[...].astype(F32)).astype(BF16)
    to_left[...] = (left_low[...].astype(F32) + via_left[...].astype(F32)).astype(BF16)


def pair_kernel(a, b, out):
    out[...] = (a[...].astype(F32) + b[...].astype(F32)).astype(BF16)


def four_sum(parts):
    a, b, c, d = [part[...].astype(F32) for part in parts]
    return (a + c) + (b + d)


def four_kernel(a, b, c, d, out):
    out[...] = four_sum((a, b, c, d)).astype(BF16)


def last_kernel(a, b, c, d, down, up):
    total = four_sum((a, b, c, d))
    down[...] = total[0:16]
    up[...] = 2.0 * total[16:32]


def finish_kernel(before, from_left, from_right, out):
    out[0:256, :] = (before[0:256, :].astype(F32) + from_left[...].astype(F32)).astype(BF16)
    out[256:512, :] = (before[256:512, :].astype(F32) + from_right[...].astype(F32)).astype(BF16)


def own_back_kernel(
    grad_in, weight, down, lora_back, from_right, from_left, out, buffer, sems, grad, in_sems
):
    arriving = [move(grad_in, grad, in_sems, s) for s in range(4)]
    fetch = Fetch(weight, buffer, sems, 0)
    local = dot(lora_back[...], down_rows(down, 0), ((0,), (0,)))
    for copy in arriving:
        copy.wait()
    for k in range(4):
        fetch.wait(k)
        lanes = slice(k * 256, k * 256 + 256)
        own = local[:, lanes] + dot(grad[...], buffer[k * 256 : k * 256 + 256, :], ((1,), (1,)))
        out[0:256, lanes] = (own[0:256] + from_right[:, lanes].astype(F32)).astype(BF16)
        out[256:512, lanes] = (own[256:512] + from_left[:, lanes].astype(F32)).astype(BF16)


def query_kernel(
    recv, home, extras, batch, pooled, qown, arrived, gradient, loss, listed
):
    group = lax.rem(lax.axis_index("dp"), 4) * 32
    place = iota((128, 1024), 0) == (iota((128, 1024), 1) & 31) + group
    place = place.astype(F32).astype(BF16)
    spread = iota((32, 1024), 0) == (iota((32, 1024), 1) >> 5)
    sub = iota((32, 128), 0)

    def by_slot(lanes):
        table = jnp.zeros((32, 128), F32)
        for d in range(32):
            table = jnp.where(sub == d, recv[d, :, lanes], table)
        wide = jnp.zeros((32, 1024), F32)
        for part in split3(table):
            wide += dot(part.astype(BF16), place, ((1,), (0,)))
        return jnp.sum(jnp.where(spread, wide, 0.0), axis=0, keepdims=True)

    score, pre = by_slot(slice(1024, 1152)), by_slot(slice(1152, 1280))
    mine, first, used = home[0:32, :], home[33:34, :], home[34:35, :] > 0.0
    log_col = extras[:, 0:1]
    log_slot = jnp.sum(mine * log_col, axis=0, keepdims=True)
    coef = jnp.where(used, LOSS_SCALE * (jnp.exp(score - log_slot) - first), 0.0)
    value = jnp.where(used, coef * pre, 0.0).astype(BF16).astype(F32)
    score = jnp.where(used, score, 0.0)
    positive = jnp.sum(mine * (first * score), axis=1, keepdims=True)
    scalar = jnp.sum(mine * (coef * score), axis=1, keepdims=True)
    scalar = scalar + jnp.sum(extras[:, 256:384], axis=1, keepdims=True)
    eye = iota((32, 128), 0) == iota((32, 128), 1)
    row = jnp.sum(jnp.where(eye, log_col - positive, 0.0), axis=0, keepdims=True)
    loss[...] = row[:, 0:32]
    qinv = batch[:, 768:769]
    last = last_rows(arrived[:, 1024:1152], 1024)
    for c in range(4):
        rows = unfold(arrived[c * 192 : c * 192 + 192, 0:1024].astype(F32), last, c * 8)
        listed[c * 256 : c * 256 + 256, :] = rows.astype(BF16)
    total = dot((mine * value).astype(BF16), listed[...], ((1,), (0,)))
    total = total + dot(extras[:, 128:256].astype(BF16), pooled[...], ((1,), (0,)))
    gradient[...] = (total - (scalar * qinv * qinv) * qown[...].astype(F32)).astype(BF16)


ANY, HOLD, LOAD, STORE = "any", "hold", "load", "store"


def call(kernel, outs, args, scratch=(), limit=16, cost=None):
    in_specs, values, moved = [], [], []
    for place, arg in enumerate(args):
        space = pltpu.VMEM
        if isinstance(arg, tuple):
            arg, mark = arg
            space = pltpu.HBM
            if mark != ANY:
                arg = pltpu.with_memory_space_constraint(arg, pltpu.HBM)
            if mark == LOAD:
                moved.append((place, arg.shape, arg.dtype))
        values.append(arg)
        in_specs.append(pl.BlockSpec(memory_space=space))
    loads = len(moved)
    for place, (shape, dtype, *mark) in enumerate(outs):
        if mark == [STORE]:
            moved.append((len(args) + place, shape, dtype))
    count, extra = len(args) + len(outs), len(moved)

    def whole(*refs):
        refs = list(refs)
        if not extra:
            return kernel(*refs)
        sems = refs.pop()
        buffers = [refs.pop() for _ in range(extra)][::-1]
        copies = []
        for i, (place, _, _) in enumerate(moved):
            ends = (refs[place], buffers[i]) if i < loads else (buffers[i], refs[place])
            copies.append(pltpu.make_async_copy(*ends, sems.at[i]))
            refs[place] = buffers[i]
        for copy in copies[:loads]:
            copy.start()
        for copy in copies[:loads]:
            copy.wait()
        kernel(*refs)
        for copy in copies[loads:]:
            copy.start()
        for copy in copies[loads:]:
            copy.wait()

    scratch = list(scratch)
    if extra:
        scratch += [pltpu.VMEM(shape, dtype) for _, shape, dtype in moved]
        scratch.append(pltpu.SemaphoreType.DMA((extra,)))
    if cost is not None:
        cost = pl.CostEstimate(flops=int(cost * 1.15e9), bytes_accessed=0, transcendentals=0)
    return pl.pallas_call(
        whole,
        cost_estimate=cost,
        name=kernel.__name__,
        out_shape=[
            (pltpu.HBM if mark else jax.ShapeDtypeStruct)(s, t) for s, t, *mark in outs
        ],
        in_specs=in_specs,
        out_specs=[
            pl.BlockSpec(memory_space=pltpu.HBM if mark else pltpu.VMEM) for _, _, *mark in outs
        ],
        scratch_shapes=scratch,
        compiler_params=pltpu.CompilerParams(vmem_limit_bytes=limit * 2**20),
    )(*values)


COST_OWN = 15.0
COST_PAIR = 3.0
COST_JOIN = 16.0
COST_GRAD = 1.0
COST_FAR = 4.0
COST_SIDES = 1.0
WEIGHT_BUFFER = pltpu.VMEM((1024, 1024), BF16)
FOUR = pltpu.SemaphoreType.DMA((4,))


def ring(x, step):
    return lax.ppermute(x, "mp", [(i, (i + step) % 4) for i in range(4)])


def ring_sum(x):
    return (x + ring(x, 2)) + (ring(x, 1) + ring(x, 3))


def grid_index(x, y, core):
    return (x * 4 + y) * 2 + core


def grid_shift(v, axis, step):
    pairs = []
    for x in range(4):
        for y in range(4):
            for core in range(2):
                if axis == "core":
                    to = (x, y, 1 - core)
                elif axis == "x":
                    to = ((x + step) % 4, y, core)
                else:
                    to = (x, (y + step) % 4, core)
                pairs.append((grid_index(x, y, core), grid_index(*to)))
    return lax.ppermute(v, "dp", pairs)


def grid_sum(x, own, query):
    shape = x.shape
    tie = lax.optimization_barrier
    (x,) = call(pair_kernel, [(shape, BF16)], [x, grid_shift(x, "core", 1)], cost=COST_PAIR)
    parts = [x] + [grid_shift(x, "x", step) for step in (1, 2, 3)]
    own, *parts = tie((own, *parts))
    (x,) = call(four_kernel, [(shape, BF16)], parts)
    parts = [x] + [grid_shift(x, "y", step) for step in (1, 2, 3)]
    query, own, *parts = tie((query, own, *parts))
    down, up = call(last_kernel, [((16, 1024), F32), ((16, 1024), F32)], parts)
    return down, up, own, query


def body(
    attention_output,
    residual,
    output_projection_weight,
    adapter_down_matrix,
    adapter_up_matrix,
    final_norm_gain,
    query_hidden_states,
    pair_passage_index,
    lengths,
):
    weight = (output_projection_weight, HOLD)
    down = adapter_down_matrix.T
    up = adapter_up_matrix
    qown = query_hidden_states
    half, full = (256, 1024), (512, 1024)
    tie = lax.optimization_barrier

    top, low = call(
        order_kernel, [(half, BF16), (half, BF16)], [(attention_output, LOAD)]
    )
    with jax.named_scope("leg1"):
        left_top, right_low = ring(top, 1), ring(low, 3)

    ids, _, _ = tie((pair_passage_index, top, low))
    flat = jnp.pad(ids.reshape(-1), (0, 640 - 544), constant_values=-1)
    qslot_out, home = call(
        slot_kernel,
        [((768, 1280), BF16, STORE), ((40, 1024), F32, STORE)],
        [flat.reshape(1, 640), flat.reshape(640, 1), qown],
    )
    with jax.named_scope("a2a_queries"):
        qslot = lax.all_to_all(qslot_out, "dp", 0, 0, tiled=True)
    with jax.named_scope("leg2"):
        left_low, right_top = ring(low, 1), ring(top, 3)
    with jax.named_scope("leg3"):
        far_top, far_low = ring(left_top, 1), ring(right_low, 3)

    residual_tied, left_top, right_low = tie((residual, left_top, right_low))
    stream, middle = call(
        own_kernel,
        [(full, F32), ((16, 512), F32)],
        [top, low, residual_tied, weight, down],
        [WEIGHT_BUFFER, FOUR], limit=24, cost=COST_OWN,
    )
    stream, middle = call(
        sides_kernel,
        [(full, F32, STORE), ((16, 512), F32)],
        [left_top, left_low, right_top, right_low, stream, middle, weight, down],
        [WEIGHT_BUFFER, WEIGHT_BUFFER, FOUR, FOUR], limit=24,
    )
    gain = final_norm_gain.astype(F32).reshape(1, 1024)
    stream, middle, tokens, table = call(
        far_kernel,
        [(full, F32, ANY), ((16, 512), BF16), (full, BF16), ((16, 128), F32)],
        [far_top, far_low, (stream, HOLD), middle, weight, down, up, gain],
        [WEIGHT_BUFFER, FOUR, pltpu.VMEM(full, F32), FOUR, pltpu.VMEM(full, F32), FOUR],
        limit=24,
        cost=COST_FAR,
    )
    qslot, table = tie((qslot, table))
    qslot, meta, turned = call(
        meta_kernel,
        [((1024, 1152), BF16), ((40, 1024), F32), ((1024, 1024), BF16)],
        [(qslot, HOLD)],
        [
            pltpu.VMEM((768, 1152), BF16), pltpu.VMEM((768, 128), BF16),
            pltpu.SemaphoreType.DMA((5,)),
        ],
    )
    (pack,) = call(partial_kernel, [((24, 1024), F32)], [tokens, turned, qown, meta, table])
    with jax.named_scope("packs"):
        packs = [pack, ring(pack, 1), ring(pack, 2), ring(pack, 3)]
    slot, batch, stats, sums = call(
        score_kernel,
        [((8, 1024), F32), ((32, 896), F32), ((16, 128), F32), ((32, 1, 1280), F32)],
        [*packs, meta, lengths.reshape(1, 128)],
    )
    with jax.named_scope("a2a_sums"):
        recv = lax.all_to_all(sums, "dp", 0, 0, tiled=True)
    pooled, rows = call(
        pooled_kernel,
        [((128, 1024), BF16), ((768, 1152), BF16)],
        [(stream, HOLD), stats, gain, qslot],
        [pltpu.VMEM(full, F32), FOUR],
    )
    grad, far_top, far_low, lora, extras, up_part = call(
        gradient_kernel,
        [
            (full, BF16, ANY), (half, BF16), (half, BF16), ((16, 512), F32),
            ((32, 384), F32, ANY), ((16, 1024), F32),
        ],
        [recv, (stream, HOLD), qslot, qown, gain, meta, slot, batch, stats, pooled, up, middle, weight],
        [
            WEIGHT_BUFFER, FOUR, pltpu.VMEM(full, F32), FOUR, pltpu.VMEM(full, BF16), FOUR,
            pltpu.VMEM((32, 384), F32), pltpu.SemaphoreType.DMA((1,)), pltpu.VMEM(full, BF16),
        ],
        limit=24, cost=COST_GRAD,
    )

    far_top, far_low, rows = tie((far_top, far_low, rows))
    with jax.named_scope("back1"):
        via_right, via_left = ring(far_top, 1), ring(far_low, 3)
    with jax.named_scope("lora_sum"):
        loras = [lora, ring(lora, 1), ring(lora, 2), ring(lora, 3)]
    with jax.named_scope("a2a_rows"):
        arrived = lax.all_to_all(rows, "dp", 0, 0, tiled=True)
    right_low, left_top, right_top, left_low = call(
        sides_back_kernel,
        [(half, BF16), (half, BF16), (half, BF16), (half, BF16)],
        [(grad, ANY), weight],
        [WEIGHT_BUFFER, WEIGHT_BUFFER, FOUR, FOUR, pltpu.VMEM(full, BF16), FOUR],
        limit=24,
        cost=COST_SIDES,
    )
    with jax.named_scope("back2"):
        to_right_low, to_left_top = ring(right_low, 1), ring(left_top, 3)
    right_top, left_low = call(
        add_kernel,
        [(half, BF16), (half, BF16)],
        [right_top, left_low, via_right, via_left],
    )
    right_top, left_low, up_part = tie((right_top, left_low, up_part))
    adapter, lora_back = call(
        join_kernel,
        [((32, 1024), BF16), ((16, 512), BF16)],
        [*loras, (attention_output, LOAD), up_part],
        cost=COST_JOIN,
    )
    with jax.named_scope("back3"):
        to_right_top, to_left_low = ring(right_top, 1), ring(left_low, 3)
    (before,) = call(
        own_back_kernel,
        [(full, BF16)],
        [(grad, ANY), weight, down, lora_back, to_left_top, to_right_low],
        [WEIGHT_BUFFER, FOUR, pltpu.VMEM(full, BF16), FOUR],
        limit=24,
    )
    query_gradient, loss = call(
        query_kernel,
        [((32, 1024), BF16), ((1, 32), F32)],
        [
            (recv, LOAD), (home, LOAD), (extras, LOAD), (batch, LOAD), (pooled, LOAD),
            (qown, LOAD), arrived,
        ],
        [pltpu.VMEM((1024, 1024), BF16)],
    )
    with jax.named_scope("adapters"):
        down_grad, up_grad, before, query_gradient = grid_sum(adapter, before, query_gradient)
    (attention_gradient,) = call(
        finish_kernel,
        [(full, BF16)],
        [before, to_right_top, to_left_low],
    )
    return (
        loss.reshape(32),
        query_gradient,
        grad,
        attention_gradient,
        down_grad.T,
        up_grad,
    )


def solution(mesh):
    in_specs = (
        P("dp", "mp"),
        P("dp", "mp"),
        P(None, "mp"),
        P(),
        P(None, "mp"),
        P("mp"),
        P("dp", "mp"),
        P("dp", None),
        P("dp"),
    )
    out_specs = (P("dp"), P("dp", "mp"), P("dp", "mp"), P("dp", "mp"), P("mp", None), P(None, "mp"))
    return jax.shard_map(body, mesh=mesh, in_specs=in_specs, out_specs=out_specs, check_vma=False)
```
